32 devices in a mesh: groups: 2 (over y), ep: 8 (over z, x), tp: 2 (over core).
Axes of the slice: x: 2, y: 2, z: 4, core: 2. Of those that a mesh axis runs over, the one named last changes fastest.
Arguments:
- partials: bfloat16 [2, 1024, 3840], P('tp', ('groups', 'ep')), parts along dimension 1, may hold values from -6 to 6
- residual: bfloat16 [1024, 3840], P(('groups', 'ep')), parts along dimension 0, may hold values from -6 to 6
- norm_gain: float32 [3840], replicated, may hold values from 0.1 to 1.9
- router_logits: float32 [1024, 8], P(('groups', 'ep')), parts along dimension 0, may hold values from -8 to 8
- expert_ids: int32 [1024, 8], P(('groups', 'ep')), parts along dimension 0, may hold values from 0 to 7, as said below
- gate_packed: float32 [8, 640, 1024], P('ep', None, 'tp'), may hold values from 0 to 16777215
- up_packed: float32 [8, 640, 1024], P('ep', None, 'tp'), may hold values from 0 to 16777215, as said below
- down_packed: float32 [8, 640, 1024], P('ep', 'tp'), may hold values from 0 to 16777215, as said below
- gate_scale: float32 [8, 1024], P('ep', 'tp'), may hold values from 0.5 to 2
- up_scale: float32 [8, 1024], P('ep', 'tp'), may hold values from 0.5 to 2
- down_scale: float32 [8, 3840], P('ep', 'tp'), may hold values from 1 to 6
Outputs:
- mixed: bfloat16 [1024, 3840], P(('groups', 'ep', 'tp')), parts along dimension 0
The draws below stay inside these ranges and needn't reach their ends.
There are 2 independent parts, one for each index of `groups`. The reference program is written for one: setup_inputs(seed, part) draws one part's arguments, and reference() takes and returns one part's arrays. A program takes and returns all parts, laid end to end along the dimension named above; an argument that names none is the same for every part. Nothing has to cross between parts.
Inputs may be any that keep to these rules, and one draw needn't show every extreme that they name: `expert_ids`: the 8 experts of a row differ. In each aligned block of 32 rows every expert that the block names is named by exactly 32 of its rows, and one expert, drawn afresh for each part, is named in every block. `up_packed`: whole numbers. `down_packed`: whole numbers.
All inputs are finite; a program needn't handle non-finite values.
Results may differ from the reference program's by a relative error of at most 0.017.
Values may be sent and summed in bfloat16 or wider, within the bound.
No kernel may reach another device: no remote copies, remote signals or barrier semaphores. Data moves between devices by JAX's collectives and lax.ppermute only.
A program may use at most 128 MiB of HBM per device.

```python
import math
import jax
import jax.numpy as jnp
from jax import lax

D = 3840
FF = 1024
TOP = 8
HB = 128
EXPERTS = 8
ROW_DEV = 32
CAP = 32
TOKENS = 512
N_TP = 2


def draw_expert_ids(key, part):
    key = jax.random.fold_in(key, 11)
    hot_key, block_key = jax.random.split(key)
    hot_expert = jax.random.randint(hot_key, (), 0, EXPERTS).astype(jnp.int32)
    spacing = ROW_DEV // CAP
    group_count = ROW_DEV * TOP // CAP
    block_count = TOKENS // ROW_DEV
    row_ids = jnp.arange(ROW_DEV, dtype=jnp.int32)[:, None]
    pick_ids = jnp.arange(TOP, dtype=jnp.int32)[None, :]
    group_of = (row_ids + pick_ids * spacing) % group_count

    def one_block(block_index):
        block_seed = jax.random.fold_in(block_key, block_index)
        expert_seed, row_seed = jax.random.split(block_seed)
        others = jax.random.permutation(expert_seed, EXPERTS - 1).astype(jnp.int32)
        others = others + (others >= hot_expert).astype(jnp.int32)
        chosen = jnp.concatenate([hot_expert[None], others[:group_count - 1]])
        pick_table = chosen[group_of]
        row_order = jax.random.permutation(row_seed, ROW_DEV)
        return pick_table[row_order]
    table = jax.vmap(one_block)(jnp.arange(block_count, dtype=jnp.int32))
    return table.reshape(TOKENS, TOP).astype(jnp.int32)


def packed_words(key):
    words = jax.random.randint(key, (EXPERTS, D // 6, FF), 0, 16777216).astype(jnp.float32)
    words = words.at[0, 0, 0].set(16777215.0)
    words = words.at[0, 0, 1].set(0.0)
    return words


def draw_gate_packed(key, part):
    key = jax.random.fold_in(key, 21)
    return packed_words(key)


def draw_up_packed(key, part):
    key = jax.random.fold_in(key, 22)
    return packed_words(key)


def draw_down_packed(key, part):
    key = jax.random.fold_in(key, 23)
    return packed_words(key)


def level_of(rng, shape, cuts, least, largest):
    factor_of = 1.0
    for dim, shards_of in cuts:
        heights = jax.random.uniform(jax.random.fold_in(jax.random.fold_in(rng, 6), dim), (shards_of,), jnp.float32, least / len(cuts), largest / len(cuts))
        factor_of = factor_of * jnp.repeat(jnp.exp(heights), shape[dim] // shards_of).reshape((-1,) + (1,) * (len(shape) - 1 - dim))
    return factor_of


def normal_values(stream_key, shape, scale, limit, pieces=(), kind=jnp.bfloat16):
    factor_of = level_of(stream_key, shape, pieces, -0.22, 0.18) if pieces else 1.0
    entries = jax.random.normal(stream_key, shape, jnp.float32) * scale * factor_of
    return jnp.minimum(jnp.maximum(entries, -limit), limit).astype(kind)


def setup_inputs(seed: int = 0, part: int = 0) -> dict:
    key_list = jax.random.split(jax.random.key(seed), 12)
    own_keys = jax.random.split(jax.random.fold_in(key_list[11], part), 12)
    return {
        "partials": normal_values(own_keys[0], (N_TP, TOKENS, D), 1.0, 6.0, ((0, 2), (1, 8))),
        "residual": normal_values(own_keys[1], (TOKENS, D), 1.0, 6.0, ((0, 8),)),
        "norm_gain": jnp.clip(1.0 + 0.18 * jax.random.normal(key_list[2], (D,), jnp.float32), 0.1, 1.9),
        "router_logits": normal_values(own_keys[3], (TOKENS, TOP), 2.0, 8.0, ((0, 8),), jnp.float32),
        "expert_ids": draw_expert_ids(jax.random.fold_in(jax.random.fold_in(key_list[11], part), 71), part),
        "gate_packed": draw_gate_packed(jax.random.fold_in(key_list[11], 71), part),
        "up_packed": draw_up_packed(jax.random.fold_in(key_list[11], 71), part),
        "down_packed": draw_down_packed(jax.random.fold_in(key_list[11], 71), part),
        "gate_scale": jnp.clip(jnp.exp(math.log(2.0) - 1.3862944 * jax.random.uniform(key_list[8], (EXPERTS, FF), jnp.float32) ** level_of(key_list[8], (EXPERTS, FF), ((0, 8), (1, 2)), -0.2, 0.2)), 0.5, 2.0),
        "up_scale": jnp.clip(jnp.exp(math.log(2.0) - 1.3862944 * jax.random.uniform(key_list[9], (EXPERTS, FF), jnp.float32) ** level_of(key_list[9], (EXPERTS, FF), ((0, 8), (1, 2)), -0.2, 0.2)), 0.5, 2.0),
        "down_scale": jnp.clip(jnp.exp(math.log(6.0) - 1.7917595 * jax.random.uniform(key_list[10], (EXPERTS, D), jnp.float32) ** level_of(key_list[10], (EXPERTS, D), ((0, 8), (1, 2)), -0.2, 0.2)), 1.0, 6.0),
    }


level_variance = 21.25

def hadamard(table_order):
    indices = jnp.arange(table_order, dtype=jnp.int32)
    common_bits = jnp.bitwise_and(indices[:, None], indices[None, :])
    parity = jnp.zeros((table_order, table_order), jnp.int32)
    for bit_pos in range(table_order.bit_length() - 1):
        parity = parity + jnp.bitwise_and(jnp.right_shift(common_bits, bit_pos), 1)
    sign_table = 1 - 2 * (parity % 2)
    return sign_table.astype(jnp.float32) * (1.0 / math.sqrt(table_order))

def rotate_blocks(values, hadamard_table):
    feature_count = values.shape[-1]
    block_size = hadamard_table.shape[0]
    shaped = values.reshape(values.shape[:-1] + (feature_count // block_size, block_size))
    turned = jnp.einsum('rij,jk->rik', shaped, hadamard_table, precision=lax.Precision.HIGHEST)
    return turned.reshape(values.shape)

def unpack_levels(packed):
    powers = jnp.array([1.0, 16.0, 256.0, 4096.0, 65536.0, 1048576.0], jnp.float32)
    digits = jnp.mod(jnp.floor(packed[:, None, :] / powers[None, :, None]), 16.0)
    levels = digits - 7.5
    return levels.reshape((packed.shape[0] * 6, packed.shape[1])).astype(jnp.bfloat16)

def prepare(stream, norm_gain, hadamard_table):
    mean_square = lax.optimization_barrier(jnp.mean(stream * stream, axis=-1, keepdims=True))
    normed = stream * lax.rsqrt(mean_square + 1e-06) * norm_gain
    return rotate_blocks(normed, hadamard_table).astype(jnp.bfloat16)

def route_weights(router_logits):
    lifted = jax.nn.sigmoid(router_logits)
    return lifted / lax.optimization_barrier(jnp.sum(lifted, axis=-1, keepdims=True))

def block_slots(expert_ids, block_rows, expert_count):
    expert_range = jnp.arange(expert_count, dtype=jnp.int32)
    member = lax.optimization_barrier(jnp.sum((expert_ids[:, :, None] == expert_range[None, None, :]).astype(jnp.int32), axis=1))
    blocks = member.reshape(-1, block_rows, expert_count)
    before = (jnp.cumsum(blocks, axis=1) - blocks).reshape(-1, expert_count)
    return jnp.take_along_axis(before, expert_ids, axis=1).astype(jnp.int32)

def expert_math(row_block, gate_levels, up_levels, down_levels, gate_row, up_row, down_row, hadamard_table):
    feature_count = row_block.shape[1]
    hidden_count = down_levels.shape[1]
    gate_proj = jnp.dot(row_block, gate_levels, preferred_element_type=jnp.float32) * (gate_row * (1.0 / math.sqrt(level_variance * feature_count)))
    up_proj = jnp.dot(row_block, up_levels, preferred_element_type=jnp.float32) * (up_row * (1.0 / math.sqrt(level_variance * feature_count)))
    hidden = rotate_blocks(jax.nn.silu(gate_proj) * up_proj, hadamard_table).astype(jnp.bfloat16)
    expert_out = lax.dot_general(hidden, down_levels, (((1,), (1,)), ((), ())), preferred_element_type=jnp.float32) * (down_row * (1.0 / math.sqrt(level_variance * hidden_count)))
    return expert_out.astype(jnp.bfloat16)

def reference(partials, residual, norm_gain, router_logits, expert_ids, gate_packed, up_packed, down_packed, gate_scale, up_scale, down_scale):
    hadamard_table = hadamard(HB)
    stream = residual.astype(jnp.float32) + lax.optimization_barrier(jnp.sum(partials.astype(jnp.float32), axis=0))
    rotated = prepare(stream, norm_gain, hadamard_table)
    weights = route_weights(router_logits)
    slot_rank = block_slots(expert_ids, ROW_DEV, EXPERTS)
    token_ids = jnp.arange(TOKENS, dtype=jnp.int32)
    group_slots = TOKENS // ROW_DEV * CAP
    position = (token_ids // ROW_DEV)[:, None] * CAP + slot_rank
    padded = jnp.concatenate([rotated, jnp.zeros((1, D), jnp.bfloat16)], axis=0)
    token_grid = jnp.broadcast_to(token_ids[:, None], expert_ids.shape).reshape(-1)
    flat_weights = weights.reshape(-1)

    def one_expert(mixture, expert):
        chosen = expert_ids == expert
        target = jnp.where(chosen, position, group_slots).reshape(-1).astype(jnp.int32)
        row_of = jnp.full((group_slots,), TOKENS, jnp.int32).at[target].set(token_grid, mode='drop')
        weight_of = jnp.zeros((group_slots,), jnp.float32).at[target].set(flat_weights, mode='drop')
        row_block = padded[row_of]
        gate_levels = unpack_levels(gate_packed[expert])
        up_levels = unpack_levels(up_packed[expert])
        down_levels = unpack_levels(down_packed[expert])
        produced = expert_math(row_block, gate_levels, up_levels, down_levels, gate_scale[expert], up_scale[expert], down_scale[expert], hadamard_table)
        mixture = mixture.at[row_of].add(weight_of[:, None] * produced.astype(jnp.float32), mode='drop')
        return (mixture, None)
    mixture, unused = lax.scan(one_expert, jnp.zeros((TOKENS, D), jnp.float32), jnp.arange(EXPERTS, dtype=jnp.int32))
    return mixture.astype(jnp.bfloat16)
```

```python
import math

import jax
import jax.numpy as jnp
import numpy as np
from jax import lax
from jax.experimental import pallas as pl
from jax.experimental.pallas import tpu as pltpu
from jax.sharding import PartitionSpec as P

HB = 128


level_variance = 21.25
digit_powers = [1.0, 16.0, 256.0, 4096.0, 65536.0, 1048576.0]


def hadamard(table_order):
    indices = jnp.arange(table_order, dtype=jnp.int32)
    common_bits = jnp.bitwise_and(indices[:, None], indices[None, :])
    parity = jnp.zeros((table_order, table_order), jnp.int32)
    for bit_pos in range(table_order.bit_length() - 1):
        parity = parity + jnp.bitwise_and(jnp.right_shift(common_bits, bit_pos), 1)
    sign_table = 1 - 2 * (parity % 2)
    return sign_table.astype(jnp.float32) * (1.0 / math.sqrt(table_order))


def rotate_blocks(values, hadamard_table):
    feature_count = values.shape[-1]
    block_size = hadamard_table.shape[0]
    shaped = values.reshape(values.shape[:-1] + (feature_count // block_size, block_size))
    turned = jnp.einsum("rij,jk->rik", shaped, hadamard_table, precision=lax.Precision.HIGHEST)
    return turned.reshape(values.shape)


def unpack_levels(packed):
    pieces = []
    for power in digit_powers:
        digit = jnp.mod(jnp.floor(packed / power), 16.0) - 7.5
        pieces.append(digit.astype(jnp.bfloat16))
    levels = jnp.stack(pieces, axis=1)
    return levels.reshape((packed.shape[0] * 6, packed.shape[1]))


def prepare(stream, norm_gain, hadamard_table):
    mean_square = jnp.mean(stream * stream, axis=-1, keepdims=True)
    normed = stream * lax.rsqrt(mean_square + 1e-06) * norm_gain
    return rotate_blocks(normed, hadamard_table).astype(jnp.bfloat16)


def route_weights(router_logits):
    lifted = jax.nn.sigmoid(router_logits)
    return lifted / jnp.sum(lifted, axis=-1, keepdims=True)


def block_slots(expert_ids, block_rows, expert_count):
    expert_range = jnp.arange(expert_count, dtype=jnp.int32)
    member = jnp.sum(
        (expert_ids[:, :, None] == expert_range[None, None, :]).astype(jnp.int32), axis=1
    )
    blocks = member.reshape(-1, block_rows, expert_count)
    before = (jnp.cumsum(blocks, axis=1) - blocks).reshape(-1, expert_count)
    return jnp.take_along_axis(before, expert_ids, axis=1)


def place_rows(rotated, target, slot_count):
    slot_ids = jnp.arange(slot_count, dtype=jnp.int32)
    hits = (target[:, :, None] == slot_ids[None, None, :]).astype(jnp.bfloat16)
    placement = jnp.sum(hits, axis=1)
    return jnp.dot(placement.T, rotated, preferred_element_type=jnp.float32).astype(jnp.bfloat16)


def expert_rows(
    row_block, gate_levels, up_levels, down_levels, gate_row, up_row, down_row, hadamard_table
):
    feature_count = row_block.shape[1]
    gate_proj = jnp.dot(row_block, gate_levels, preferred_element_type=jnp.float32) * (
        gate_row * (1.0 / math.sqrt(level_variance * feature_count))
    )
    up_proj = jnp.dot(row_block, up_levels, preferred_element_type=jnp.float32) * (
        up_row * (1.0 / math.sqrt(level_variance * feature_count))
    )
    hidden = rotate_blocks(jax.nn.silu(gate_proj) * up_proj, hadamard_table).astype(jnp.bfloat16)
    whole_hidden = lax.all_gather(hidden, "tp", axis=1, tiled=True)
    hidden_count = whole_hidden.shape[1]
    expert_out = lax.dot_general(
        whole_hidden, down_levels, (((1,), (1,)), ((), ())), preferred_element_type=jnp.float32
    ) * (down_row * (1.0 / math.sqrt(level_variance * hidden_count)))
    return expert_out.astype(jnp.bfloat16)


def routed_shards(
    partials,
    residual,
    norm_gain,
    router_logits,
    expert_ids,
    gate_packed,
    up_packed,
    down_packed,
    gate_scale,
    up_scale,
    down_scale,
):
    tp_count = lax.axis_size("tp")
    ep_count = lax.axis_size("ep")
    tp_index = lax.axis_index("tp")
    block_tokens = residual.shape[0]
    half_rows = block_tokens // tp_count
    pick_count = expert_ids.shape[1]
    experts = ep_count * gate_packed.shape[0]
    capacity = max(2, half_rows * pick_count // experts)
    hadamard_table = hadamard(HB)
    gate_levels = unpack_levels(gate_packed[0])
    up_levels = unpack_levels(up_packed[0])
    down_levels = unpack_levels(down_packed[0])
    weights = route_weights(router_logits)
    slot_rank = block_slots(expert_ids, half_rows, experts)
    half_of_row = (jnp.arange(block_tokens, dtype=jnp.int32) // half_rows)[:, None]
    summed_rows = lax.psum_scatter(partials, "tp", scatter_dimension=1, tiled=True).astype(
        jnp.float32
    )
    own_resid = lax.dynamic_slice_in_dim(residual, tp_index * half_rows, half_rows, 0)
    stream = own_resid.astype(jnp.float32) + summed_rows[0]
    rotated = prepare(stream, norm_gain, hadamard_table)
    own_ids = lax.dynamic_slice_in_dim(expert_ids, tp_index * half_rows, half_rows, 0)
    own_slots = lax.dynamic_slice_in_dim(slot_rank, tp_index * half_rows, half_rows, 0)
    outgoing = place_rows(rotated, own_ids * capacity + own_slots, experts * capacity)
    outgoing = outgoing.reshape(experts, capacity, -1)
    arrived = lax.all_to_all(outgoing, "ep", split_axis=0, concat_axis=0, tiled=True)
    paired = lax.all_gather(arrived, "tp", axis=0, tiled=True)
    produced = expert_rows(
        paired.reshape(-1, paired.shape[2]),
        gate_levels,
        up_levels,
        down_levels,
        gate_scale[0],
        up_scale[0],
        down_scale[0],
        hadamard_table,
    )
    served = produced.reshape(tp_count, ep_count, arrived.shape[1], -1)
    returned = lax.all_to_all(served, "ep", split_axis=1, concat_axis=1, tiled=True)
    position = half_of_row * (experts * capacity) + expert_ids * capacity + slot_rank
    flat_back = returned.reshape(-1, returned.shape[-1])
    mixture = jnp.zeros((block_tokens, flat_back.shape[1]), jnp.float32)
    for pick in range(pick_count):
        fetched = jnp.take(flat_back, position[:, pick], axis=0)
        mixture = mixture + weights[:, pick : pick + 1] * fetched.astype(jnp.float32)
    arranged = mixture.reshape(tp_count, half_rows, -1)
    mixed = lax.all_to_all(
        arranged.astype(jnp.bfloat16), "tp", split_axis=0, concat_axis=2, tiled=True
    ).astype(arranged.dtype)
    return mixed[0].astype(jnp.bfloat16)


UNIT = 64
SPAN = 6 * UNIT
EXTRA = 128


def level_order():
    order = np.zeros((SPAN, SPAN), np.float32)
    for plane in range(6):
        for row in range(UNIT):
            order[6 * row + plane, plane * UNIT + row] = 1.0
    return order


def sign_blocks(count):
    indices = np.arange(HB)
    common = indices[:, None] & indices[None, :]
    parity = np.zeros((HB, HB), np.int64)
    for bit_pos in range(HB.bit_length() - 1):
        parity += (common >> bit_pos) & 1
    return np.kron(np.eye(count), 1.0 - 2.0 * (parity % 2)).astype(np.float32)


def fold(values, span):
    return jnp.concatenate(
        [values[:, i * span : (i + 1) * span] for i in range(values.shape[1] // span)], axis=0
    )


def unfold(values, rows):
    return jnp.concatenate(
        [values[i * rows : (i + 1) * rows] for i in range(values.shape[0] // rows)], axis=1
    )


def signed_product(values, signs):
    high = values.astype(jnp.bfloat16)
    low = (values - high.astype(jnp.float32)).astype(jnp.bfloat16)
    both = jnp.concatenate([high, low], axis=0)
    product = jnp.dot(both, signs, preferred_element_type=jnp.float32)
    rows = values.shape[0]
    return (product[:rows] + product[rows:]) * (1.0 / math.sqrt(HB))


def prep_kernel(own, other, resid, gain, logits, ids, signs, out):
    rows, features = own.shape
    stream = resid[...].astype(jnp.float32) + (
        own[...].astype(jnp.float32) + other[...].astype(jnp.float32)
    )
    mean_square = jnp.mean(stream * stream, axis=-1, keepdims=True)
    normed = stream * lax.rsqrt(mean_square + 1e-06) * gain[...]
    turned = signed_product(fold(normed, SPAN), signs[...])
    out[:, :features] = unfold(turned, rows).astype(jnp.bfloat16)
    lifted = jax.nn.sigmoid(logits[...])
    route = lifted / jnp.sum(lifted, axis=-1, keepdims=True)
    picks = route.shape[1]
    lane = lax.broadcasted_iota(jnp.int32, (rows, EXTRA), 1)
    spread = jnp.zeros((rows, EXTRA), jnp.float32)
    for pick in range(picks):
        hit = (lane & (picks - 1)) == ids[:, pick : pick + 1]
        spread = spread + jnp.where(hit, route[:, pick : pick + 1], 0.0)
    high = spread.astype(jnp.bfloat16).astype(jnp.float32)
    tail = jnp.where(lane < picks, high, jnp.where(lane < 2 * picks, spread - high, 0.0))
    out[:, features:] = tail.astype(jnp.bfloat16)


def unpack_block(words, out, columns):
    whole = words.astype(jnp.int32)
    for plane in range(6):
        digit = jnp.bitwise_and(jnp.right_shift(whole, 4 * plane), 15)
        level = digit.astype(jnp.float32) - 7.5
        out[plane * UNIT : (plane + 1) * UNIT, columns] = level.astype(jnp.bfloat16)


def unpack_in_kernel(gate, up, gate_out, up_out):
    unpack_block(gate[...], gate_out, slice(None))
    unpack_block(up[...], up_out, slice(None))


def unpack_in(gate_packed, up_packed):
    packed_rows, columns = gate_packed.shape
    in_spec = pl.BlockSpec((UNIT, columns), lambda i: (i, 0))
    out_spec = pl.BlockSpec((SPAN, columns), lambda i: (i, 0))
    shape = jax.ShapeDtypeStruct((6 * packed_rows, columns), jnp.bfloat16)
    return pl.pallas_call(
        unpack_in_kernel,
        grid=(packed_rows // UNIT,),
        in_specs=[in_spec, in_spec],
        out_specs=[out_spec, out_spec],
        out_shape=[shape, shape],
        name="unpack_in",
    )(gate_packed, up_packed)


def unpack_down_kernel(place, mine, theirs, out):
    half = mine.shape[1]
    unpack_block(mine[...], out, slice(0, half))
    unpack_block(theirs[...], out, slice(half, 2 * half))


def unpack_down(place, down_packed):
    packed_rows, columns = down_packed.shape
    half = columns // 2
    return pl.pallas_call(
        unpack_down_kernel,
        grid_spec=pltpu.PrefetchScalarGridSpec(
            num_scalar_prefetch=1,
            grid=(packed_rows // UNIT,),
            in_specs=[
                pl.BlockSpec((UNIT, half), lambda i, place: (i, place[0])),
                pl.BlockSpec((UNIT, half), lambda i, place: (i, 1 - place[0])),
            ],
            out_specs=pl.BlockSpec((SPAN, columns), lambda i, place: (i, 0)),
        ),
        out_shape=jax.ShapeDtypeStruct((6 * packed_rows, columns), jnp.bfloat16),
        name="unpack_down",
    )(place, down_packed, down_packed)


def hidden_kernel(count, place, *refs):
    pieces, (gate, up, gate_row, up_row, signs, hidden, weight, rows_ref) = (
        refs[: 2 * count],
        refs[2 * count :],
    )
    half, width = pieces[0].shape
    features = width - EXTRA
    lane = lax.broadcasted_iota(jnp.int32, (half, EXTRA), 1)
    picked = (lane < 16) & ((lane & 7) == place[1])
    for index in range(count):
        for side in range(2):
            core = place[0] if side == 0 else 1 - place[0]
            at = pl.ds(pl.multiple_of(2 * half * index + core * half, half), half)
            piece = pieces[2 * index + side]
            rows_ref[at, :] = piece[:, :features]
            tail = jnp.where(picked, piece[:, features:].astype(jnp.float32), 0.0)
            total = jnp.sum(tail, axis=-1, keepdims=True)
            weight[at, :] = jnp.broadcast_to(total, (half, EXTRA))
    scale = 1.0 / math.sqrt(level_variance * features)
    rows = rows_ref[...]
    gate_proj = jnp.dot(rows, gate[...], preferred_element_type=jnp.float32)
    up_proj = jnp.dot(rows, up[...], preferred_element_type=jnp.float32)
    mixed = jax.nn.silu(gate_proj * (gate_row[...] * scale)) * (up_proj * (up_row[...] * scale))
    turned = signed_product(fold(mixed, 2 * HB), signs[...])
    hidden[...] = unfold(turned, mixed.shape[0]).astype(jnp.bfloat16)


def hidden_part(place, pieces, gate, up, gate_row, up_row, signs):
    count = len(pieces) // 2
    half, width = pieces[0].shape
    rows = 2 * half * count
    vmem = pl.BlockSpec(memory_space=pltpu.VMEM)
    return pl.pallas_call(
        lambda *refs: hidden_kernel(count, *refs),
        in_specs=[pl.BlockSpec(memory_space=pltpu.SMEM)] + [vmem] * (len(pieces) + 5),
        out_specs=[vmem, vmem],
        out_shape=[
            jax.ShapeDtypeStruct((rows, gate.shape[1]), jnp.bfloat16),
            jax.ShapeDtypeStruct((rows, EXTRA), jnp.float32),
        ],
        scratch_shapes=[pltpu.VMEM((rows, width - EXTRA), jnp.bfloat16)],
        compiler_params=pltpu.CompilerParams(vmem_limit_bytes=40 << 20),
        name="hidden_part",
    )(place, *pieces, gate, up, gate_row, up_row, signs)


def down_kernel(mine, theirs, levels, down_row, weight, *outs):
    half = mine.shape[1]
    contract = (((1,), (1,)), ((), ()))
    produced = lax.dot_general(
        mine[...], levels[:, :half], contract, preferred_element_type=jnp.float32
    ) + lax.dot_general(
        theirs[...], levels[:, half:], contract, preferred_element_type=jnp.float32
    )
    scale = 1.0 / math.sqrt(level_variance * 2 * half)
    produced = produced * (down_row[...] * scale) * weight[:, :1]
    rows = outs[0].shape[0]
    for index, out in enumerate(outs):
        out[...] = produced[index * rows : (index + 1) * rows]


def down_part(mine, theirs, levels, down_row, weight, count):
    rows = mine.shape[0] // count
    vmem = pl.BlockSpec(memory_space=pltpu.VMEM)
    return pl.pallas_call(
        down_kernel,
        in_specs=[vmem] * 5,
        out_specs=[vmem] * count,
        out_shape=[jax.ShapeDtypeStruct((rows, levels.shape[0]), jnp.float32)] * count,
        compiler_params=pltpu.CompilerParams(vmem_limit_bytes=40 << 20),
        name="down_part",
    )(mine, theirs, levels, down_row, weight)


def close_kernel(own, left, right, order, out):
    total = own[...] + left[...].astype(jnp.float32) + right[...].astype(jnp.float32)
    rows = total.shape[0]
    folded = fold(total.astype(jnp.bfloat16), SPAN)
    placed = jnp.dot(folded, order[...], preferred_element_type=jnp.float32)
    out[...] = unfold(placed, rows).astype(jnp.bfloat16)


def whole_call(kernel, shape, name, *args):
    vmem = pl.BlockSpec(memory_space=pltpu.VMEM)
    return pl.pallas_call(
        kernel,
        in_specs=[vmem] * len(args),
        out_specs=vmem,
        out_shape=shape,
        compiler_params=pltpu.CompilerParams(vmem_limit_bytes=40 << 20),
        name=name,
    )(*args)


def dense_shards(
    partials,
    residual,
    norm_gain,
    router_logits,
    expert_ids,
    gate_packed,
    up_packed,
    down_packed,
    gate_scale,
    up_scale,
    down_scale,
):
    ep_count = lax.axis_size("ep")
    tp_index = lax.axis_index("tp")
    ep_index = lax.axis_index("ep")
    block_rows, features = residual.shape
    half = block_rows // 2
    place = jnp.stack([tp_index, ep_index]).astype(jnp.int32)

    around = list(range(0, ep_count, 2)) + list(range(ep_count - 1, 0, -2))

    def device(spot, core):
        return around[spot % ep_count] * 2 + core

    def hop(values, step):
        pairs = [(device(s, c), device(s + step, c)) for s in range(ep_count) for c in range(2)]
        return lax.ppermute(values, ("ep", "tp"), pairs)

    def swap(values):
        return lax.ppermute(values, "tp", [(0, 1), (1, 0)])

    def own_half(values, other=False):
        at = (1 - tp_index if other else tp_index) * half
        return lax.dynamic_slice_in_dim(values, at, half, 0)

    turn = sign_blocks(SPAN // HB) @ level_order()
    turn = jnp.asarray(turn, jnp.bfloat16)
    turn_hidden = jnp.asarray(sign_blocks(2), jnp.bfloat16)
    back = jnp.asarray(level_order().T, jnp.bfloat16)

    other_sum = swap(own_half(partials[0], other=True))
    rows = whole_call(
        prep_kernel,
        jax.ShapeDtypeStruct((half, features + EXTRA), jnp.bfloat16),
        "prep",
        own_half(partials[0]),
        other_sum,
        own_half(residual),
        norm_gain[None],
        own_half(router_logits),
        own_half(expert_ids),
        turn,
    )

    gate, up = unpack_in(gate_packed[0], up_packed[0])
    down = unpack_down(place, down_packed[0])
    down_row = down_scale[0].reshape(-1, UNIT, 6).transpose(0, 2, 1).reshape(1, -1)

    def expert_hidden(pieces):
        both = []
        for piece in pieces:
            both += [piece, swap(piece)]
        return hidden_part(place, both, gate, up, gate_scale, up_scale, turn_hidden)

    def expert_out(hidden, weight, count):
        return down_part(hidden, swap(hidden), down, down_row, weight, count)

    far = ep_count // 2
    stages = [expert_hidden([rows])]
    onward, backward = rows, rows
    for _ in range(1, far):
        onward, backward = hop(onward, 1), hop(backward, -1)
        stages.append(expert_hidden([onward, backward]))
    quarter = half // 2
    last = jnp.concatenate([hop(onward[:quarter], 1), hop(backward[quarter:], -1)], axis=0)
    stages.append(expert_hidden([last]))

    def join(part, came):
        return (part + came.astype(jnp.float32)).astype(jnp.bfloat16)

    (edge,) = expert_out(*stages[far], 1)
    edge = edge.astype(jnp.bfloat16)
    ahead, behind = hop(edge[:half], 1), hop(edge[half:], -1)
    for distance in range(far - 1, 0, -1):
        part_behind, part_ahead = expert_out(*stages[distance], 2)
        if distance == far - 1:
            send_ahead = jnp.concatenate(
                [join(part_ahead[:half], ahead), part_ahead[half:].astype(jnp.bfloat16)], axis=0
            )
            send_behind = jnp.concatenate(
                [part_behind[:half].astype(jnp.bfloat16), join(part_behind[half:], behind)], axis=0
            )
        else:
            send_ahead, send_behind = join(part_ahead, ahead), join(part_behind, behind)
        ahead, behind = hop(send_ahead, 1), hop(send_behind, -1)
    (own,) = expert_out(*stages[0], 1)
    mixed = whole_call(
        close_kernel,
        jax.ShapeDtypeStruct(own.shape, jnp.bfloat16),
        "close",
        own,
        ahead,
        behind,
        back,
    )
    mine, theirs = own_half(mixed), swap(own_half(mixed, other=True))
    first = jnp.where(tp_index == 0, mine, theirs)
    second = jnp.where(tp_index == 0, theirs, mine)
    return jnp.concatenate([first, second], axis=1)


def solution(mesh):
    def shards(*args):
        experts = lax.axis_size("ep") * args[5].shape[0]
        every_row_everywhere = args[4].shape[1] == experts
        one_each = args[5].shape[0] == 1 and lax.axis_size("tp") == 2
        if every_row_everywhere and one_each and lax.axis_size("ep") == 8:
            return dense_shards(*args)
        return routed_shards(*args)

    return jax.shard_map(
        shards,
        mesh=mesh,
        in_specs=(
            P("tp", ("groups", "ep"), None),
            P(("groups", "ep"), None),
            P(),
            P(("groups", "ep"), None),
            P(("groups", "ep"), None),
            P("ep", None, "tp"),
            P("ep", None, "tp"),
            P("ep", "tp", None),
            P("ep", "tp"),
            P("ep", "tp"),
            P("ep", "tp"),
        ),
        out_specs=P(("groups", "ep", "tp"), None),
        check_vma=False,
    )
```

```python
import math

import jax
import jax.numpy as jnp
import numpy as np
from jax import lax
from jax.experimental import pallas as pl
from jax.experimental.pallas import tpu as pltpu
from jax.sharding import PartitionSpec as P

HB = 128


level_variance = 21.25
digit_powers = [1.0, 16.0, 256.0, 4096.0, 65536.0, 1048576.0]


def hadamard(table_order):
    indices = jnp.arange(table_order, dtype=jnp.int32)
    common_bits = jnp.bitwise_and(indices[:, None], indices[None, :])
    parity = jnp.zeros((table_order, table_order), jnp.int32)
    for bit_pos in range(table_order.bit_length() - 1):
        parity = parity + jnp.bitwise_and(jnp.right_shift(common_bits, bit_pos), 1)
    sign_table = 1 - 2 * (parity % 2)
    return sign_table.astype(jnp.float32) * (1.0 / math.sqrt(table_order))


def rotate_blocks(values, hadamard_table):
    feature_count = values.shape[-1]
    block_size = hadamard_table.shape[0]
    shaped = values.reshape(values.shape[:-1] + (feature_count // block_size, block_size))
    turned = jnp.einsum("rij,jk->rik", shaped, hadamard_table, precision=lax.Precision.HIGHEST)
    return turned.reshape(values.shape)


def unpack_levels(packed):
    pieces = []
    for power in digit_powers:
        digit = jnp.mod(jnp.floor(packed / power), 16.0) - 7.5
        pieces.append(digit.astype(jnp.bfloat16))
    levels = jnp.stack(pieces, axis=1)
    return levels.reshape((packed.shape[0] * 6, packed.shape[1]))


def prepare(stream, norm_gain, hadamard_table):
    mean_square = jnp.mean(stream * stream, axis=-1, keepdims=True)
    normed = stream * lax.rsqrt(mean_square + 1e-06) * norm_gain
    return rotate_blocks(normed, hadamard_table).astype(jnp.bfloat16)


def route_weights(router_logits):
    lifted = jax.nn.sigmoid(router_logits)
    return lifted / jnp.sum(lifted, axis=-1, keepdims=True)


def block_slots(expert_ids, block_rows, expert_count):
    expert_range = jnp.arange(expert_count, dtype=jnp.int32)
    member = jnp.sum(
        (expert_ids[:, :, None] == expert_range[None, None, :]).astype(jnp.int32), axis=1
    )
    blocks = member.reshape(-1, block_rows, expert_count)
    before = (jnp.cumsum(blocks, axis=1) - blocks).reshape(-1, expert_count)
    return jnp.take_along_axis(before, expert_ids, axis=1)


def place_rows(rotated, target, slot_count):
    slot_ids = jnp.arange(slot_count, dtype=jnp.int32)
    hits = (target[:, :, None] == slot_ids[None, None, :]).astype(jnp.bfloat16)
    placement = jnp.sum(hits, axis=1)
    return jnp.dot(placement.T, rotated, preferred_element_type=jnp.float32).astype(jnp.bfloat16)


def expert_rows(
    row_block, gate_levels, up_levels, down_levels, gate_row, up_row, down_row, hadamard_table
):
    feature_count = row_block.shape[1]
    gate_proj = jnp.dot(row_block, gate_levels, preferred_element_type=jnp.float32) * (
        gate_row * (1.0 / math.sqrt(level_variance * feature_count))
    )
    up_proj = jnp.dot(row_block, up_levels, preferred_element_type=jnp.float32) * (
        up_row * (1.0 / math.sqrt(level_variance * feature_count))
    )
    hidden = rotate_blocks(jax.nn.silu(gate_proj) * up_proj, hadamard_table).astype(jnp.bfloat16)
    whole_hidden = lax.all_gather(hidden, "tp", axis=1, tiled=True)
    hidden_count = whole_hidden.shape[1]
    expert_out = lax.dot_general(
        whole_hidden, down_levels, (((1,), (1,)), ((), ())), preferred_element_type=jnp.float32
    ) * (down_row * (1.0 / math.sqrt(level_variance * hidden_count)))
    return expert_out.astype(jnp.bfloat16)


def routed_shards(
    partials,
    residual,
    norm_gain,
    router_logits,
    expert_ids,
    gate_packed,
    up_packed,
    down_packed,
    gate_scale,
    up_scale,
    down_scale,
):
    tp_count = lax.axis_size("tp")
    ep_count = lax.axis_size("ep")
    tp_index = lax.axis_index("tp")
    block_tokens = residual.shape[0]
    half_rows = block_tokens // tp_count
    pick_count = expert_ids.shape[1]
    experts = ep_count * gate_packed.shape[0]
    capacity = max(2, half_rows * pick_count // experts)
    hadamard_table = hadamard(HB)
    gate_levels = unpack_levels(gate_packed[0])
    up_levels = unpack_levels(up_packed[0])
    down_levels = unpack_levels(down_packed[0])
    weights = route_weights(router_logits)
    slot_rank = block_slots(expert_ids, half_rows, experts)
    half_of_row = (jnp.arange(block_tokens, dtype=jnp.int32) // half_rows)[:, None]
    summed_rows = lax.psum_scatter(partials, "tp", scatter_dimension=1, tiled=True).astype(
        jnp.float32
    )
    own_resid = lax.dynamic_slice_in_dim(residual, tp_index * half_rows, half_rows, 0)
    stream = own_resid.astype(jnp.float32) + summed_rows[0]
    rotated = prepare(stream, norm_gain, hadamard_table)
    own_ids = lax.dynamic_slice_in_dim(expert_ids, tp_index * half_rows, half_rows, 0)
    own_slots = lax.dynamic_slice_in_dim(slot_rank, tp_index * half_rows, half_rows, 0)
    outgoing = place_rows(rotated, own_ids * capacity + own_slots, experts * capacity)
    outgoing = outgoing.reshape(experts, capacity, -1)
    arrived = lax.all_to_all(outgoing, "ep", split_axis=0, concat_axis=0, tiled=True)
    paired = lax.all_gather(arrived, "tp", axis=0, tiled=True)
    produced = expert_rows(
        paired.reshape(-1, paired.shape[2]),
        gate_levels,
        up_levels,
        down_levels,
        gate_scale[0],
        up_scale[0],
        down_scale[0],
        hadamard_table,
    )
    served = produced.reshape(tp_count, ep_count, arrived.shape[1], -1)
    returned = lax.all_to_all(served, "ep", split_axis=1, concat_axis=1, tiled=True)
    position = half_of_row * (experts * capacity) + expert_ids * capacity + slot_rank
    flat_back = returned.reshape(-1, returned.shape[-1])
    mixture = jnp.zeros((block_tokens, flat_back.shape[1]), jnp.float32)
    for pick in range(pick_count):
        fetched = jnp.take(flat_back, position[:, pick], axis=0)
        mixture = mixture + weights[:, pick : pick + 1] * fetched.astype(jnp.float32)
    arranged = mixture.reshape(tp_count, half_rows, -1)
    mixed = lax.all_to_all(
        arranged.astype(jnp.bfloat16), "tp", split_axis=0, concat_axis=2, tiled=True
    ).astype(arranged.dtype)
    return mixed[0].astype(jnp.bfloat16)


UNIT = 64
SPAN = 6 * UNIT
ALONE = ((0, None, 1), (0, None, 0))
ROUND = ((0, 0, 1), (0, 1, 0), (0, 0, 0), (0, 1, 1))
NEAR = ALONE + tuple((slot + 1, place, half) for slot, place, half in ROUND)
EXTRA = 128


def level_order():
    order = np.zeros((SPAN, SPAN), np.float32)
    for plane in range(6):
        for row in range(UNIT):
            order[6 * row + plane, plane * UNIT + row] = 1.0
    return order


def sign_blocks(count):
    indices = np.arange(HB)
    common = indices[:, None] & indices[None, :]
    parity = np.zeros((HB, HB), np.int64)
    for bit_pos in range(HB.bit_length() - 1):
        parity += (common >> bit_pos) & 1
    return np.kron(np.eye(count), 1.0 - 2.0 * (parity % 2)).astype(np.float32)


def fold(values, span):
    return jnp.concatenate(
        [values[:, i * span : (i + 1) * span] for i in range(values.shape[1] // span)], axis=0
    )


def unfold(values, rows):
    return jnp.concatenate(
        [values[i * rows : (i + 1) * rows] for i in range(values.shape[0] // rows)], axis=1
    )


def signed_product(values, signs):
    high = values.astype(jnp.bfloat16)
    low = (values - high.astype(jnp.float32)).astype(jnp.bfloat16)
    both = jnp.concatenate([high, low], axis=0)
    product = jnp.dot(both, signs, preferred_element_type=jnp.float32)
    rows = values.shape[0]
    return (product[:rows] + product[rows:]) * (1.0 / math.sqrt(HB))


def core_of(side):
    core = lax.axis_index("tp")
    return core if side == 0 else 1 - core


def own_rows(half, core):
    return pl.ds(pl.multiple_of(core * half, half), half)


def first_kernel(
    partial,
    resid,
    gain,
    signs,
    all_logits,
    all_ids,
    words,
    base,
    gain_out,
    signs_out,
    tail,
    words_out,
    rows_in,
    logits,
    ids,
    sems,
):
    copies = [
        pltpu.make_async_copy(partial, rows_in.at[0], sems.at[0]),
        pltpu.make_async_copy(resid, rows_in.at[1], sems.at[1]),
        pltpu.make_async_copy(gain, gain_out, sems.at[2]),
        pltpu.make_async_copy(signs, signs_out, sems.at[3]),
    ]
    small = [
        pltpu.make_async_copy(all_logits, logits, sems.at[4]),
        pltpu.make_async_copy(all_ids, ids, sems.at[5]),
    ]
    later = pltpu.make_async_copy(words, words_out, sems.at[6])
    for copy in small + copies + [later]:
        copy.start()
    for copy in small:
        copy.wait()
    lifted = jax.nn.sigmoid(logits[...])
    route = lifted / jnp.sum(lifted, axis=0, keepdims=True)
    picks, rows = route.shape
    expert = lax.broadcasted_iota(jnp.int32, (picks, rows), 0)
    spread = jnp.zeros((picks, rows), jnp.float32)
    for pick in range(picks):
        hit = expert == ids[pick : pick + 1, :]
        spread = spread + jnp.where(hit, route[pick : pick + 1, :], 0.0)
    high = spread.astype(jnp.bfloat16).astype(jnp.float32)
    blank = jnp.zeros((EXTRA - 2 * picks, rows), jnp.float32)
    columns = jnp.concatenate([high, spread - high, blank], axis=0)
    tail[...] = columns.T.astype(jnp.bfloat16)
    for copy in copies:
        copy.wait()
    base[...] = rows_in[1].astype(jnp.float32) + rows_in[0].astype(jnp.float32)
    later.wait()


def prep_kernel(side, base, other, gain, signs, tail, out):
    rows, features = out.shape[0], base.shape[1]
    at = own_rows(rows, core_of(side))
    stream = base[at, :] + other[at, :].astype(jnp.float32)
    mean_square = jnp.mean(stream * stream, axis=-1, keepdims=True)
    normed = stream * lax.rsqrt(mean_square + 1e-06) * gain[...].reshape(1, features)
    turned = signed_product(fold(normed, SPAN), signs[...])
    out[:, :features] = unfold(turned, rows).astype(jnp.bfloat16)
    out[:, features:] = tail[at, :]


def unpack_unit(words, out, at, columns):
    whole = words.astype(jnp.int32)
    for plane in range(6):
        digit = jnp.bitwise_and(jnp.right_shift(whole, 4 * plane), 15)
        level = digit.astype(jnp.float32) - 7.5
        out[pl.ds(at + plane * UNIT, UNIT), columns] = level.astype(jnp.bfloat16)


def unpack_all(packed, out, parts):
    def unit(index, carry):
        for source, columns in parts:
            words = packed[pl.ds(pl.multiple_of(index * UNIT, UNIT), UNIT), source]
            unpack_unit(words, out, pl.multiple_of(index * SPAN, SPAN), columns)
        return carry

    lax.fori_loop(0, packed.shape[0] // UNIT, unit, 0)


def unpack_gate_kernel(up, down, gate, out, up_out, down_out, sems):
    copies = [
        pltpu.make_async_copy(up, up_out, sems.at[0]),
        pltpu.make_async_copy(down, down_out, sems.at[1]),
    ]
    for copy in copies:
        copy.start()
    unpack_all(gate, out, ((slice(None), slice(None)),))
    for copy in copies:
        copy.wait()


def unpack_up_kernel(up, out):
    unpack_all(up, out, ((slice(None), slice(None)),))


def unpack_down_kernel(down, scale, order, out, row):
    half = down.shape[1] // 2
    core = lax.axis_index("tp")
    mine = pl.ds(pl.multiple_of(core * half, half), half)
    theirs = pl.ds(pl.multiple_of((1 - core) * half, half), half)
    unpack_all(down, out, ((mine, slice(0, half)), (theirs, slice(half, 2 * half))))
    rest = fold(jnp.broadcast_to(scale[...], (8, scale.shape[1])), SPAN)
    total = jnp.zeros(rest.shape, jnp.float32)
    for _ in range(3):
        term = rest.astype(jnp.bfloat16)
        rest = rest - term.astype(jnp.float32)
        total = total + jnp.dot(term, order[...], preferred_element_type=jnp.float32)
    row[...] = unfold(total, 8)


def slot_row(count, slot, side, part):
    at = slot if side is None else slot + core_of(side)
    return (2 * at + core_of(part)) * count


def hidden_kernel(slots, *refs):
    pieces, (gate, up, gate_row, up_row, signs, hidden, weight, rows_ref) = (
        refs[: len(slots)],
        refs[len(slots) :],
    )
    features = gate.shape[0]
    picks = lax.axis_size("ep")
    for piece, (slot, side, part) in zip(pieces, slots):
        count = piece.shape[0]
        lane = lax.broadcasted_iota(jnp.int32, (count, EXTRA), 1)
        picked = (lane < 2 * picks) & ((lane & (picks - 1)) == lax.axis_index("ep"))
        row = slot_row(count, slot, side, part)
        at = pl.ds(pl.multiple_of(row, count), count)
        rows_ref[at, :] = piece[:, :features]
        tail = jnp.where(picked, piece[:, features:].astype(jnp.float32), 0.0)
        total = jnp.sum(tail, axis=-1, keepdims=True)
        weight[at, :] = jnp.broadcast_to(total, (count, EXTRA))
    scale = 1.0 / math.sqrt(level_variance * features)
    rows = rows_ref[...]
    gate_proj = jnp.dot(rows, gate[...], preferred_element_type=jnp.float32)
    up_proj = jnp.dot(rows, up[...], preferred_element_type=jnp.float32)
    gate_proj, up_proj = gate_proj[: hidden.shape[0]], up_proj[: hidden.shape[0]]
    mixed = jax.nn.silu(gate_proj * (gate_row[...] * scale)) * (up_proj * (up_row[...] * scale))
    turned = signed_product(fold(mixed, 2 * HB), signs[...])
    hidden[...] = unfold(turned, mixed.shape[0])[: hidden.shape[0]].astype(jnp.bfloat16)


def down_kernel(mine, theirs, levels, down_row, weight, *outs):
    half = mine.shape[1]
    contract = (((1,), (1,)), ((), ()))
    produced = lax.dot_general(
        mine[...], levels[:, :half], contract, preferred_element_type=jnp.float32
    ) + lax.dot_general(
        theirs[...], levels[:, half:], contract, preferred_element_type=jnp.float32
    )
    scale = 1.0 / math.sqrt(level_variance * 2 * half)
    produced = produced * (down_row[:1, :] * scale) * weight[:, :1]
    rows = outs[0].shape[0]
    for index, out in enumerate(outs):
        out[...] = produced[index * rows : (index + 1) * rows]


def close_kernel(own, ahead, behind, order, out):
    total = own[...] + (ahead[...].astype(jnp.float32) + behind[...].astype(jnp.float32))
    folded = fold(total.astype(jnp.bfloat16), SPAN)
    placed = jnp.dot(folded, order[...], preferred_element_type=jnp.float32)
    out[...] = unfold(placed, total.shape[0]).astype(jnp.bfloat16)


def on_chip(values):
    return pltpu.with_memory_space_constraint(values, pltpu.VMEM)


def whole_call(
    kernel, outs, name, *args, scratch=(), work=0, after=None, fetched=0, plain=False
):
    vmem = pl.BlockSpec(memory_space=pltpu.VMEM)
    specs = [pl.BlockSpec(memory_space=pltpu.HBM)] * fetched + [vmem] * (len(args) - fetched)
    stay = [pltpu.with_memory_space_constraint(a, pltpu.HBM) for a in args[:fetched]]
    args = (*stay, *args[fetched:])
    body = kernel
    if after is not None:
        specs, args = [pl.BlockSpec(memory_space=pl.ANY)] + specs, (after, *args)
        body = lambda first, *refs: kernel(*refs)
    return pl.pallas_call(
        body,
        in_specs=specs,
        out_specs=[vmem] * len(outs),
        out_shape=[(jax.ShapeDtypeStruct if plain else pltpu.VMEM)(*out) for out in outs],
        scratch_shapes=list(scratch),
        compiler_params=pltpu.CompilerParams(vmem_limit_bytes=12 << 20),
        cost_estimate=pl.CostEstimate(flops=work, bytes_accessed=0, transcendentals=0),
        name=name,
    )(*args)


def dense_shards(
    partials,
    residual,
    norm_gain,
    router_logits,
    expert_ids,
    gate_packed,
    up_packed,
    down_packed,
    gate_scale,
    up_scale,
    down_scale,
):
    ep_count = lax.axis_size("ep")
    tp_index = lax.axis_index("tp")
    block_rows, features = residual.shape
    half = block_rows // 2
    around = list(range(0, ep_count, 2)) + list(range(ep_count - 1, 0, -2))

    def device(spot, core):
        return around[spot % ep_count] * 2 + core

    def hop(values):
        spots = range(ep_count)
        pairs = [(device(s, 0), device(s + 1, 0)) for s in spots]
        pairs += [(device(s, 1), device(s - 1, 1)) for s in spots]
        return lax.ppermute(values, ("ep", "tp"), pairs)

    def turn_hop(values, step):
        pairs = [(device(s, c), device(s + step, c)) for s in range(ep_count) for c in range(2)]
        return lax.ppermute(values, ("ep", "tp"), pairs)

    def swap(values):
        return lax.ppermute(values, "tp", [(0, 1), (1, 0)])

    def own_half(values, other=False):
        at = (1 - tp_index if other else tp_index) * half
        return lax.dynamic_slice_in_dim(values, at, half, 0)

    turn = sign_blocks(SPAN // HB) @ level_order()
    turn = jnp.asarray(turn, jnp.bfloat16)
    turn_hidden = jnp.asarray(sign_blocks(2), jnp.bfloat16)
    order = jnp.asarray(level_order(), jnp.bfloat16)
    back = jnp.asarray(level_order().T, jnp.bfloat16)

    wide = features + EXTRA
    first = whole_call(
        first_kernel,
        [
            ((block_rows, features), jnp.float32),
            (norm_gain.shape, jnp.float32),
            (turn.shape, turn.dtype),
            ((block_rows, EXTRA), jnp.bfloat16),
            (gate_packed.shape[1:], jnp.float32),
        ],
        "first",
        partials[0],
        residual,
        norm_gain,
        turn,
        router_logits.T,
        expert_ids.T,
        gate_packed[0],
        fetched=7,
        scratch=[
            pltpu.VMEM((2, block_rows, features), jnp.bfloat16),
            pltpu.VMEM(router_logits.T.shape, jnp.float32),
            pltpu.VMEM(expert_ids.T.shape, jnp.int32),
            pltpu.SemaphoreType.DMA((7,)),
        ],
    )
    base, gain, turn, tail, gate_words = first
    other_partial = swap(partials[0])

    def prepared(side, after=None):
        (rows,) = whole_call(
            lambda *refs: prep_kernel(side, *refs),
            [((half, wide), jnp.bfloat16)],
            "prep",
            base,
            other_partial,
            gain,
            turn,
            tail,
            after=after,
        )
        return rows

    lead = [prepared(1)]
    follow = [prepared(0, after=lead[0])]

    packed_rows, columns = gate_packed.shape[1:]

    levels = ((6 * packed_rows, columns), jnp.bfloat16)
    gate, up_words, down_words = whole_call(
        unpack_gate_kernel,
        [levels, (up_packed.shape[1:], jnp.float32), (down_packed.shape[1:], jnp.float32)],
        "unpack_gate",
        up_packed[0],
        down_packed[0],
        on_chip(gate_words),
        fetched=2,
        scratch=[pltpu.SemaphoreType.DMA((2,))],
        after=follow[0],
        work=10**10,
    )
    down_rows, hidden_count = down_packed.shape[1:]
    down_features = 6 * down_rows

    def hold(values, *done):
        return lax.optimization_barrier((values, done))[0]

    def expert_hidden(pieces, slots, count, work=10**9):
        hidden, weight = whole_call(
            lambda *refs: hidden_kernel(slots, *refs),
            [
                ((block_rows * count, columns), jnp.bfloat16),
                ((block_rows * count, EXTRA), jnp.float32),
            ],
            "hidden_part",
            *pieces,
            on_chip(gate),
            on_chip(up),
            gate_scale,
            up_scale,
            turn_hidden,
            scratch=[pltpu.VMEM((max(2, count) * block_rows, features), jnp.bfloat16)],
            work=work,
        )
        return hidden, weight, swap(hidden)

    def expert_out(stage, after=None):
        hidden, weight, theirs = stage
        count = hidden.shape[0] // block_rows
        return whole_call(
            down_kernel,
            [((block_rows, down_features), jnp.float32)] * count,
            "down_part",
            hidden,
            theirs,
            on_chip(down),
            down_row,
            weight,
            work=2 * block_rows * count * hidden_count * down_features,
            after=after,
        )

    lead.append(hop(lead[0]))
    follow.append(hop(follow[0]))
    (up,) = whole_call(
        unpack_up_kernel, [levels], "unpack_up", on_chip(up_words), after=gate, work=10**10
    )
    lead[1] = hold(lead[1], gate)
    lead.append(hop(lead[1]))
    follow.append(hop(follow[1]))
    lead[2] = hold(lead[2], up)
    down, down_row = whole_call(
        unpack_down_kernel,
        [((down_features, hidden_count), jnp.bfloat16), ((8, down_features), jnp.float32)],
        "unpack_down",
        on_chip(down_words),
        down_scale,
        order,
        after=up,
        work=10**10,
    )
    lead.append(hop(lead[2]))
    follow.append(hop(follow[2]))
    lead[3] = hold(lead[3], down_row)
    lead.append(hop(lead[3]))

    def pieces(distance):
        ours = lead[distance], follow[distance]
        return [piece for own in ours for piece in (own, swap(own))]

    lead[2], follow[2] = hold(lead[2], down_row), hold(follow[2], down_row)
    lead.append(hop(lead[2]))
    follow.append(hop(follow[2]))
    beside = pieces(3)
    near = expert_hidden(hold([lead[0], follow[0]] + pieces(1), beside[1]), NEAR, 3, work=10**10)
    second = expert_hidden(hold(pieces(2), beside[1]), ROUND, 2, work=10**10)
    third = expert_hidden(beside, ROUND, 2, work=10**9)
    lead[4] = hold(lead[4], near[1], second[1])
    edge = expert_hidden(hold([lead[4], swap(lead[4])], third[1]), ALONE, 1, work=10**9)

    far = ep_count // 2

    def join(part, came):
        return (part + came.astype(jnp.float32)).astype(jnp.bfloat16)

    ahead, behind = {}, {}
    behind[3], ahead[3] = expert_out(third)
    (edge,) = expert_out(edge, after=ahead[3])
    went_ahead = turn_hop(edge[:half].astype(jnp.bfloat16), 1)
    went_behind = turn_hop(edge[half:].astype(jnp.bfloat16), -1)
    behind[2], ahead[2] = expert_out(second, after=went_behind)
    own, behind[1], ahead[1] = expert_out(near, after=went_behind)
    for distance in range(far - 1, 0, -1):
        if distance == far - 1:
            send_ahead = jnp.concatenate(
                [
                    join(ahead[distance][:half], went_ahead),
                    ahead[distance][half:].astype(jnp.bfloat16),
                ],
                axis=0,
            )
            send_behind = jnp.concatenate(
                [
                    behind[distance][:half].astype(jnp.bfloat16),
                    join(behind[distance][half:], went_behind),
                ],
                axis=0,
            )
        else:
            send_ahead = join(ahead[distance], went_ahead)
            send_behind = join(behind[distance], went_behind)
        went_ahead, went_behind = turn_hop(send_ahead, 1), turn_hop(send_behind, -1)
    (mixed,) = whole_call(
        close_kernel,
        [(own.shape, jnp.bfloat16)],
        "close",
        own,
        went_ahead,
        went_behind,
        back,
    )
    mine, theirs = own_half(mixed), swap(own_half(mixed, other=True))
    first = jnp.where(tp_index == 0, mine, theirs)
    second = jnp.where(tp_index == 0, theirs, mine)
    return jnp.concatenate([first, second], axis=1)


def solution(mesh):
    def shards(*args):
        experts = lax.axis_size("ep") * args[5].shape[0]
        every_row_everywhere = args[4].shape[1] == experts
        one_each = args[5].shape[0] == 1 and lax.axis_size("tp") == 2
        if every_row_everywhere and one_each and lax.axis_size("ep") == 8:
            return dense_shards(*args)
        return routed_shards(*args)

    return jax.shard_map(
        shards,
        mesh=mesh,
        in_specs=(
            P("tp", ("groups", "ep"), None),
            P(("groups", "ep"), None),
            P(),
            P(("groups", "ep"), None),
            P(("groups", "ep"), None),
            P("ep", None, "tp"),
            P("ep", None, "tp"),
            P("ep", "tp", None),
            P("ep", "tp"),
            P("ep", "tp"),
            P("ep", "tp"),
        ),
        out_specs=P(("groups", "ep", "tp"), None),
        check_vma=False,
    )
```

```python
import math

import jax
import jax.numpy as jnp
import numpy as np
from jax import lax
from jax.experimental import pallas as pl
from jax.experimental.pallas import tpu as pltpu
from jax.sharding import PartitionSpec as P

HB = 128


level_variance = 21.25
digit_powers = [1.0, 16.0, 256.0, 4096.0, 65536.0, 1048576.0]


def hadamard(table_order):
    indices = jnp.arange(table_order, dtype=jnp.int32)
    common_bits = jnp.bitwise_and(indices[:, None], indices[None, :])
    parity = jnp.zeros((table_order, table_order), jnp.int32)
    for bit_pos in range(table_order.bit_length() - 1):
        parity = parity + jnp.bitwise_and(jnp.right_shift(common_bits, bit_pos), 1)
    sign_table = 1 - 2 * (parity % 2)
    return sign_table.astype(jnp.float32) * (1.0 / math.sqrt(table_order))


def rotate_blocks(values, hadamard_table):
    feature_count = values.shape[-1]
    block_size = hadamard_table.shape[0]
    shaped = values.reshape(values.shape[:-1] + (feature_count // block_size, block_size))
    turned = jnp.einsum("rij,jk->rik", shaped, hadamard_table, precision=lax.Precision.HIGHEST)
    return turned.reshape(values.shape)


def unpack_levels(packed):
    pieces = []
    for power in digit_powers:
        digit = jnp.mod(jnp.floor(packed / power), 16.0) - 7.5
        pieces.append(digit.astype(jnp.bfloat16))
    levels = jnp.stack(pieces, axis=1)
    return levels.reshape((packed.shape[0] * 6, packed.shape[1]))


def prepare(stream, norm_gain, hadamard_table):
    mean_square = jnp.mean(stream * stream, axis=-1, keepdims=True)
    normed = stream * lax.rsqrt(mean_square + 1e-06) * norm_gain
    return rotate_blocks(normed, hadamard_table).astype(jnp.bfloat16)


def route_weights(router_logits):
    lifted = jax.nn.sigmoid(router_logits)
    return lifted / jnp.sum(lifted, axis=-1, keepdims=True)


def block_slots(expert_ids, block_rows, expert_count):
    expert_range = jnp.arange(expert_count, dtype=jnp.int32)
    member = jnp.sum(
        (expert_ids[:, :, None] == expert_range[None, None, :]).astype(jnp.int32), axis=1
    )
    blocks = member.reshape(-1, block_rows, expert_count)
    before = (jnp.cumsum(blocks, axis=1) - blocks).reshape(-1, expert_count)
    return jnp.take_along_axis(before, expert_ids, axis=1)


def place_rows(rotated, target, slot_count):
    slot_ids = jnp.arange(slot_count, dtype=jnp.int32)
    hits = (target[:, :, None] == slot_ids[None, None, :]).astype(jnp.bfloat16)
    placement = jnp.sum(hits, axis=1)
    return jnp.dot(placement.T, rotated, preferred_element_type=jnp.float32).astype(jnp.bfloat16)


def expert_rows(
    row_block, gate_levels, up_levels, down_levels, gate_row, up_row, down_row, hadamard_table
):
    feature_count = row_block.shape[1]
    gate_proj = jnp.dot(row_block, gate_levels, preferred_element_type=jnp.float32) * (
        gate_row * (1.0 / math.sqrt(level_variance * feature_count))
    )
    up_proj = jnp.dot(row_block, up_levels, preferred_element_type=jnp.float32) * (
        up_row * (1.0 / math.sqrt(level_variance * feature_count))
    )
    hidden = rotate_blocks(jax.nn.silu(gate_proj) * up_proj, hadamard_table).astype(jnp.bfloat16)
    whole_hidden = lax.all_gather(hidden, "tp", axis=1, tiled=True)
    hidden_count = whole_hidden.shape[1]
    expert_out = lax.dot_general(
        whole_hidden, down_levels, (((1,), (1,)), ((), ())), preferred_element_type=jnp.float32
    ) * (down_row * (1.0 / math.sqrt(level_variance * hidden_count)))
    return expert_out.astype(jnp.bfloat16)


def routed_shards(
    partials,
    residual,
    norm_gain,
    router_logits,
    expert_ids,
    gate_packed,
    up_packed,
    down_packed,
    gate_scale,
    up_scale,
    down_scale,
):
    tp_count = lax.axis_size("tp")
    ep_count = lax.axis_size("ep")
    tp_index = lax.axis_index("tp")
    block_tokens = residual.shape[0]
    half_rows = block_tokens // tp_count
    pick_count = expert_ids.shape[1]
    experts = ep_count * gate_packed.shape[0]
    capacity = max(2, half_rows * pick_count // experts)
    hadamard_table = hadamard(HB)
    gate_levels = unpack_levels(gate_packed[0])
    up_levels = unpack_levels(up_packed[0])
    down_levels = unpack_levels(down_packed[0])
    weights = route_weights(router_logits)
    slot_rank = block_slots(expert_ids, half_rows, experts)
    half_of_row = (jnp.arange(block_tokens, dtype=jnp.int32) // half_rows)[:, None]
    summed_rows = lax.psum_scatter(partials, "tp", scatter_dimension=1, tiled=True).astype(
        jnp.float32
    )
    own_resid = lax.dynamic_slice_in_dim(residual, tp_index * half_rows, half_rows, 0)
    stream = own_resid.astype(jnp.float32) + summed_rows[0]
    rotated = prepare(stream, norm_gain, hadamard_table)
    own_ids = lax.dynamic_slice_in_dim(expert_ids, tp_index * half_rows, half_rows, 0)
    own_slots = lax.dynamic_slice_in_dim(slot_rank, tp_index * half_rows, half_rows, 0)
    outgoing = place_rows(rotated, own_ids * capacity + own_slots, experts * capacity)
    outgoing = outgoing.reshape(experts, capacity, -1)
    arrived = lax.all_to_all(outgoing, "ep", split_axis=0, concat_axis=0, tiled=True)
    paired = lax.all_gather(arrived, "tp", axis=0, tiled=True)
    produced = expert_rows(
        paired.reshape(-1, paired.shape[2]),
        gate_levels,
        up_levels,
        down_levels,
        gate_scale[0],
        up_scale[0],
        down_scale[0],
        hadamard_table,
    )
    served = produced.reshape(tp_count, ep_count, arrived.shape[1], -1)
    returned = lax.all_to_all(served, "ep", split_axis=1, concat_axis=1, tiled=True)
    position = half_of_row * (experts * capacity) + expert_ids * capacity + slot_rank
    flat_back = returned.reshape(-1, returned.shape[-1])
    mixture = jnp.zeros((block_tokens, flat_back.shape[1]), jnp.float32)
    for pick in range(pick_count):
        fetched = jnp.take(flat_back, position[:, pick], axis=0)
        mixture = mixture + weights[:, pick : pick + 1] * fetched.astype(jnp.float32)
    arranged = mixture.reshape(tp_count, half_rows, -1)
    mixed = lax.all_to_all(
        arranged.astype(jnp.bfloat16), "tp", split_axis=0, concat_axis=2, tiled=True
    ).astype(arranged.dtype)
    return mixed[0].astype(jnp.bfloat16)


UNIT = 64
SPAN = 6 * UNIT
APART = ((0, None, 1), (0, None, 0), (1, None, 1), (1, None, 0))
ROUND = ((0, 0, 1), (0, 1, 0), (0, 0, 0), (0, 1, 1))
EXTRA = 128


def level_order():
    order = np.zeros((SPAN, SPAN), np.float32)
    for plane in range(6):
        for row in range(UNIT):
            order[6 * row + plane, plane * UNIT + row] = 1.0
    return order


def sign_blocks(count):
    indices = np.arange(HB)
    common = indices[:, None] & indices[None, :]
    parity = np.zeros((HB, HB), np.int64)
    for bit_pos in range(HB.bit_length() - 1):
        parity += (common >> bit_pos) & 1
    return np.kron(np.eye(count), 1.0 - 2.0 * (parity % 2)).astype(np.float32)


def fold(values, span):
    return jnp.concatenate(
        [values[:, i * span : (i + 1) * span] for i in range(values.shape[1] // span)], axis=0
    )


def unfold(values, rows):
    return jnp.concatenate(
        [values[i * rows : (i + 1) * rows] for i in range(values.shape[0] // rows)], axis=1
    )


def signed_product(values, signs):
    high = values.astype(jnp.bfloat16)
    low = (values - high.astype(jnp.float32)).astype(jnp.bfloat16)
    both = jnp.concatenate([high, low], axis=0)
    product = jnp.dot(both, signs, preferred_element_type=jnp.float32)
    rows = values.shape[0]
    return (product[:rows] + product[rows:]) * (1.0 / math.sqrt(HB))


def core_of(side):
    core = lax.axis_index("tp")
    return core if side == 0 else 1 - core


def own_rows(half, core):
    return pl.ds(pl.multiple_of(core * half, half), half)


def first_kernel(
    partial,
    resid,
    gain,
    signs,
    all_logits,
    all_ids,
    words,
    base,
    gain_out,
    signs_out,
    tail,
    words_out,
    rows_in,
    logits,
    ids,
    sems,
):
    copies = [
        pltpu.make_async_copy(partial, rows_in.at[0], sems.at[0]),
        pltpu.make_async_copy(resid, rows_in.at[1], sems.at[1]),
        pltpu.make_async_copy(gain, gain_out, sems.at[2]),
        pltpu.make_async_copy(signs, signs_out, sems.at[3]),
    ]
    small = [
        pltpu.make_async_copy(all_logits, logits, sems.at[4]),
        pltpu.make_async_copy(all_ids, ids, sems.at[5]),
    ]
    later = pltpu.make_async_copy(words, words_out, sems.at[6])
    for copy in small + copies + [later]:
        copy.start()
    for copy in small:
        copy.wait()
    lifted = jax.nn.sigmoid(logits[...])
    route = lifted / jnp.sum(lifted, axis=0, keepdims=True)
    picks, rows = route.shape
    expert = lax.broadcasted_iota(jnp.int32, (picks, rows), 0)
    spread = jnp.zeros((picks, rows), jnp.float32)
    for pick in range(picks):
        hit = expert == ids[pick : pick + 1, :]
        spread = spread + jnp.where(hit, route[pick : pick + 1, :], 0.0)
    high = spread.astype(jnp.bfloat16).astype(jnp.float32)
    blank = jnp.zeros((EXTRA - 2 * picks, rows), jnp.float32)
    columns = jnp.concatenate([high, spread - high, blank], axis=0)
    tail[...] = columns.T.astype(jnp.bfloat16)
    for copy in copies:
        copy.wait()
    base[...] = rows_in[1].astype(jnp.float32) + rows_in[0].astype(jnp.float32)
    later.wait()


def prep_kernel(side, base, other, gain, signs, tail, out):
    rows, features = out.shape[0], base.shape[1]
    at = own_rows(rows, core_of(side))
    stream = base[at, :] + other[at, :].astype(jnp.float32)
    mean_square = jnp.mean(stream * stream, axis=-1, keepdims=True)
    normed = stream * lax.rsqrt(mean_square + 1e-06) * gain[...].reshape(1, features)
    turned = signed_product(fold(normed, SPAN), signs[...])
    out[:, :features] = unfold(turned, rows).astype(jnp.bfloat16)
    out[:, features:] = tail[at, :]


def unpack_unit(words, out, at, columns):
    whole = words.astype(jnp.int32)
    for plane in range(6):
        digit = jnp.bitwise_and(jnp.right_shift(whole, 4 * plane), 15)
        level = digit.astype(jnp.float32) - 7.5
        out[pl.ds(at + plane * UNIT, UNIT), columns] = level.astype(jnp.bfloat16)


def unpack_all(packed, out, parts):
    def unit(index, carry):
        for source, columns in parts:
            words = packed[pl.ds(pl.multiple_of(index * UNIT, UNIT), UNIT), source]
            unpack_unit(words, out, pl.multiple_of(index * SPAN, SPAN), columns)
        return carry

    lax.fori_loop(0, packed.shape[0] // UNIT, unit, 0)


def unpack_gate_kernel(up, down, gate, out, up_out, down_out, sems):
    copies = [
        pltpu.make_async_copy(up, up_out, sems.at[0]),
        pltpu.make_async_copy(down, down_out, sems.at[1]),
    ]
    for copy in copies:
        copy.start()
    unpack_all(gate, out, ((slice(None), slice(None)),))
    for copy in copies:
        copy.wait()


def unpack_up_kernel(up, out):
    unpack_all(up, out, ((slice(None), slice(None)),))


def unpack_down_kernel(down, scale, order, out, row):
    half = down.shape[1] // 2
    core = lax.axis_index("tp")
    mine = pl.ds(pl.multiple_of(core * half, half), half)
    theirs = pl.ds(pl.multiple_of((1 - core) * half, half), half)
    unpack_all(down, out, ((mine, slice(0, half)), (theirs, slice(half, 2 * half))))
    rest = fold(jnp.broadcast_to(scale[...], (8, scale.shape[1])), SPAN)
    total = jnp.zeros(rest.shape, jnp.float32)
    for _ in range(3):
        term = rest.astype(jnp.bfloat16)
        rest = rest - term.astype(jnp.float32)
        total = total + jnp.dot(term, order[...], preferred_element_type=jnp.float32)
    row[...] = unfold(total, 8)


def slot_row(count, slot, side, part):
    at = slot if side is None else slot + core_of(side)
    return (2 * at + core_of(part)) * count


def hidden_kernel(slots, *refs):
    pieces, (gate, up, gate_row, up_row, signs, hidden, weight, rows_ref) = (
        refs[: len(slots)],
        refs[len(slots) :],
    )
    features = gate.shape[0]
    picks = lax.axis_size("ep")
    for piece, (slot, side, part) in zip(pieces, slots):
        count = piece.shape[0]
        lane = lax.broadcasted_iota(jnp.int32, (count, EXTRA), 1)
        picked = (lane < 2 * picks) & ((lane & (picks - 1)) == lax.axis_index("ep"))
        row = slot_row(count, slot, side, part)
        at = pl.ds(pl.multiple_of(row, count), count)
        rows_ref[at, :] = piece[:, :features]
        tail = jnp.where(picked, piece[:, features:].astype(jnp.float32), 0.0)
        total = jnp.sum(tail, axis=-1, keepdims=True)
        weight[at, :] = jnp.broadcast_to(total, (count, EXTRA))
    scale = 1.0 / math.sqrt(level_variance * features)
    rows = rows_ref[...]
    gate_proj = jnp.dot(rows, gate[...], preferred_element_type=jnp.float32)
    up_proj = jnp.dot(rows, up[...], preferred_element_type=jnp.float32)
    gate_proj, up_proj = gate_proj[: hidden.shape[0]], up_proj[: hidden.shape[0]]
    mixed = jax.nn.silu(gate_proj * (gate_row[...] * scale)) * (up_proj * (up_row[...] * scale))
    turned = signed_product(fold(mixed, 2 * HB), signs[...])
    hidden[...] = unfold(turned, mixed.shape[0])[: hidden.shape[0]].astype(jnp.bfloat16)


def down_kernel(mine, theirs, levels, down_row, weight, *outs):
    half = mine.shape[1]
    contract = (((1,), (1,)), ((), ()))
    produced = lax.dot_general(
        mine[...], levels[:, :half], contract, preferred_element_type=jnp.float32
    ) + lax.dot_general(
        theirs[...], levels[:, half:], contract, preferred_element_type=jnp.float32
    )
    scale = 1.0 / math.sqrt(level_variance * 2 * half)
    produced = produced * (down_row[:1, :] * scale) * weight[:, :1]
    rows = outs[0].shape[0]
    for index, out in enumerate(outs):
        out[...] = produced[index * rows : (index + 1) * rows]


def close_kernel(own, ahead, behind, order, out):
    total = own[...] + (ahead[...].astype(jnp.float32) + behind[...].astype(jnp.float32))
    folded = fold(total.astype(jnp.bfloat16), SPAN)
    placed = jnp.dot(folded, order[...], preferred_element_type=jnp.float32)
    out[...] = unfold(placed, total.shape[0]).astype(jnp.bfloat16)


def on_chip(values):
    return pltpu.with_memory_space_constraint(values, pltpu.VMEM)


def whole_call(
    kernel, outs, name, *args, scratch=(), work=0, after=None, fetched=0, plain=False
):
    vmem = pl.BlockSpec(memory_space=pltpu.VMEM)
    specs = [pl.BlockSpec(memory_space=pltpu.HBM)] * fetched + [vmem] * (len(args) - fetched)
    stay = [pltpu.with_memory_space_constraint(a, pltpu.HBM) for a in args[:fetched]]
    args = (*stay, *args[fetched:])
    body = kernel
    if after is not None:
        specs, args = [pl.BlockSpec(memory_space=pl.ANY)] + specs, (after, *args)
        body = lambda first, *refs: kernel(*refs)
    return pl.pallas_call(
        body,
        in_specs=specs,
        out_specs=[vmem] * len(outs),
        out_shape=[(jax.ShapeDtypeStruct if plain else pltpu.VMEM)(*out) for out in outs],
        scratch_shapes=list(scratch),
        compiler_params=pltpu.CompilerParams(vmem_limit_bytes=12 << 20),
        cost_estimate=pl.CostEstimate(flops=work, bytes_accessed=0, transcendentals=0),
        name=name,
    )(*args)


def dense_shards(
    partials,
    residual,
    norm_gain,
    router_logits,
    expert_ids,
    gate_packed,
    up_packed,
    down_packed,
    gate_scale,
    up_scale,
    down_scale,
):
    ep_count = lax.axis_size("ep")
    tp_index = lax.axis_index("tp")
    block_rows, features = residual.shape
    half = block_rows // 2
    around = list(range(0, ep_count, 2)) + list(range(ep_count - 1, 0, -2))

    def device(spot, core):
        return around[spot % ep_count] * 2 + core

    def hop(values):
        spots = range(ep_count)
        pairs = [(device(s, 0), device(s + 1, 0)) for s in spots]
        pairs += [(device(s, 1), device(s - 1, 1)) for s in spots]
        return lax.ppermute(values, ("ep", "tp"), pairs)

    def turn_hop(values, step):
        pairs = [(device(s, c), device(s + step, c)) for s in range(ep_count) for c in range(2)]
        return lax.ppermute(values, ("ep", "tp"), pairs)

    def swap(values):
        return lax.ppermute(values, "tp", [(0, 1), (1, 0)])

    def own_half(values, other=False):
        at = (1 - tp_index if other else tp_index) * half
        return lax.dynamic_slice_in_dim(values, at, half, 0)

    turn = sign_blocks(SPAN // HB) @ level_order()
    turn = jnp.asarray(turn, jnp.bfloat16)
    turn_hidden = jnp.asarray(sign_blocks(2), jnp.bfloat16)
    order = jnp.asarray(level_order(), jnp.bfloat16)
    back = jnp.asarray(level_order().T, jnp.bfloat16)

    wide = features + EXTRA
    first = whole_call(
        first_kernel,
        [
            ((block_rows, features), jnp.float32),
            (norm_gain.shape, jnp.float32),
            (turn.shape, turn.dtype),
            ((block_rows, EXTRA), jnp.bfloat16),
            (gate_packed.shape[1:], jnp.float32),
        ],
        "first",
        partials[0],
        residual,
        norm_gain,
        turn,
        router_logits.T,
        expert_ids.T,
        gate_packed[0],
        fetched=7,
        scratch=[
            pltpu.VMEM((2, block_rows, features), jnp.bfloat16),
            pltpu.VMEM(router_logits.T.shape, jnp.float32),
            pltpu.VMEM(expert_ids.T.shape, jnp.int32),
            pltpu.SemaphoreType.DMA((7,)),
        ],
    )
    base, gain, turn, tail, gate_words = first
    other_partial = swap(partials[0])

    def prepared(side, after=None):
        (rows,) = whole_call(
            lambda *refs: prep_kernel(side, *refs),
            [((half, wide), jnp.bfloat16)],
            "prep",
            base,
            other_partial,
            gain,
            turn,
            tail,
            after=after,
        )
        return rows

    lead = [prepared(1)]
    follow = [prepared(0, after=lead[0])]

    packed_rows, columns = gate_packed.shape[1:]

    levels = ((6 * packed_rows, columns), jnp.bfloat16)
    gate, up_words, down_words = whole_call(
        unpack_gate_kernel,
        [levels, (up_packed.shape[1:], jnp.float32), (down_packed.shape[1:], jnp.float32)],
        "unpack_gate",
        up_packed[0],
        down_packed[0],
        on_chip(gate_words),
        fetched=2,
        scratch=[pltpu.SemaphoreType.DMA((2,))],
        after=follow[0],
        work=10**10,
    )
    down_rows, hidden_count = down_packed.shape[1:]
    down_features = 6 * down_rows

    def hold(values, *done):
        return lax.optimization_barrier((values, done))[0]

    def expert_hidden(pieces, slots, count, work=10**9):
        hidden, weight = whole_call(
            lambda *refs: hidden_kernel(slots, *refs),
            [
                ((block_rows * count, columns), jnp.bfloat16),
                ((block_rows * count, EXTRA), jnp.float32),
            ],
            "hidden_part",
            *pieces,
            on_chip(gate),
            on_chip(up),
            gate_scale,
            up_scale,
            turn_hidden,
            scratch=[pltpu.VMEM((max(2, count) * block_rows, features), jnp.bfloat16)],
            work=work,
        )
        return hidden, weight, swap(hidden)

    def expert_out(stage, after=None):
        hidden, weight, theirs = stage
        count = hidden.shape[0] // block_rows
        return whole_call(
            down_kernel,
            [((block_rows, down_features), jnp.float32)] * count,
            "down_part",
            hidden,
            theirs,
            on_chip(down),
            down_row,
            weight,
            work=2 * block_rows * count * hidden_count * down_features,
            after=after,
        )

    lead.append(hop(lead[0]))
    follow.append(hop(follow[0]))
    (up,) = whole_call(
        unpack_up_kernel, [levels], "unpack_up", on_chip(up_words), after=gate, work=10**10
    )
    lead[1] = hold(lead[1], gate)
    lead.append(hop(lead[1]))
    follow.append(hop(follow[1]))
    lead[2] = hold(lead[2], up)
    down, down_row = whole_call(
        unpack_down_kernel,
        [((down_features, hidden_count), jnp.bfloat16), ((8, down_features), jnp.float32)],
        "unpack_down",
        on_chip(down_words),
        down_scale,
        order,
        after=up,
        work=10**10,
    )
    lead.append(hop(lead[2]))
    follow.append(hop(follow[2]))

    def pieces(distance):
        ours = lead[distance], follow[distance]
        return [piece for own in ours for piece in (own, swap(own))]

    near = expert_hidden(pieces(1), ROUND, 2, work=10**9)
    lead[3] = hold(lead[3], near[1], down_row)
    lead.append(hop(lead[3]))
    beside = pieces(3)
    second = expert_hidden(hold(pieces(2), beside[1]), ROUND, 2, work=10**10)
    third = expert_hidden(beside, ROUND, 2, work=10**9)
    lead[4] = hold(lead[4], second[1], third[1])
    rows = [lead[4], swap(lead[4]), lead[0], follow[0]]
    edge = expert_hidden(hold(rows, third[1]), APART, 2, work=10**9)

    far = ep_count // 2

    def join(part, came):
        return (part + came.astype(jnp.float32)).astype(jnp.bfloat16)

    ahead, behind = {}, {}
    behind[3], ahead[3] = expert_out(third)
    edge, own = expert_out(edge, after=ahead[3])
    went_ahead = turn_hop(edge[:half].astype(jnp.bfloat16), 1)
    went_behind = turn_hop(edge[half:].astype(jnp.bfloat16), -1)
    behind[2], ahead[2] = expert_out(second, after=went_behind)
    behind[1], ahead[1] = expert_out(near, after=went_behind)
    for distance in range(far - 1, 0, -1):
        if distance == far - 1:
            send_ahead = jnp.concatenate(
                [
                    join(ahead[distance][:half], went_ahead),
                    ahead[distance][half:].astype(jnp.bfloat16),
                ],
                axis=0,
            )
            send_behind = jnp.concatenate(
                [
                    behind[distance][:half].astype(jnp.bfloat16),
                    join(behind[distance][half:], went_behind),
                ],
                axis=0,
            )
        else:
            send_ahead = join(ahead[distance], went_ahead)
            send_behind = join(behind[distance], went_behind)
        went_ahead, went_behind = turn_hop(send_ahead, 1), turn_hop(send_behind, -1)
    (mixed,) = whole_call(
        close_kernel,
        [(own.shape, jnp.bfloat16)],
        "close",
        own,
        went_ahead,
        went_behind,
        back,
    )
    mine, theirs = own_half(mixed), swap(own_half(mixed, other=True))
    first = jnp.where(tp_index == 0, mine, theirs)
    second = jnp.where(tp_index == 0, theirs, mine)
    return jnp.concatenate([first, second], axis=1)


def solution(mesh):
    def shards(*args):
        experts = lax.axis_size("ep") * args[5].shape[0]
        every_row_everywhere = args[4].shape[1] == experts
        one_each = args[5].shape[0] == 1 and lax.axis_size("tp") == 2
        if every_row_everywhere and one_each and lax.axis_size("ep") == 8:
            return dense_shards(*args)
        return routed_shards(*args)

    return jax.shard_map(
        shards,
        mesh=mesh,
        in_specs=(
            P("tp", ("groups", "ep"), None),
            P(("groups", "ep"), None),
            P(),
            P(("groups", "ep"), None),
            P(("groups", "ep"), None),
            P("ep", None, "tp"),
            P("ep", None, "tp"),
            P("ep", "tp", None),
            P("ep", "tp"),
            P("ep", "tp"),
            P("ep", "tp"),
        ),
        out_specs=P(("groups", "ep", "tp"), None),
        check_vma=False,
    )
```

```python
import math

import jax
import jax.numpy as jnp
import numpy as np
from jax import lax
from jax.experimental import pallas as pl
from jax.experimental.pallas import tpu as pltpu
from jax.sharding import PartitionSpec as P

HB = 128


level_variance = 21.25
digit_powers = [1.0, 16.0, 256.0, 4096.0, 65536.0, 1048576.0]


def hadamard(table_order):
    indices = jnp.arange(table_order, dtype=jnp.int32)
    common_bits = jnp.bitwise_and(indices[:, None], indices[None, :])
    parity = jnp.zeros((table_order, table_order), jnp.int32)
    for bit_pos in range(table_order.bit_length() - 1):
        parity = parity + jnp.bitwise_and(jnp.right_shift(common_bits, bit_pos), 1)
    sign_table = 1 - 2 * (parity % 2)
    return sign_table.astype(jnp.float32) * (1.0 / math.sqrt(table_order))


def rotate_blocks(values, hadamard_table):
    feature_count = values.shape[-1]
    block_size = hadamard_table.shape[0]
    shaped = values.reshape(values.shape[:-1] + (feature_count // block_size, block_size))
    turned = jnp.einsum("rij,jk->rik", shaped, hadamard_table, precision=lax.Precision.HIGHEST)
    return turned.reshape(values.shape)


def unpack_levels(packed):
    pieces = []
    for power in digit_powers:
        digit = jnp.mod(jnp.floor(packed / power), 16.0) - 7.5
        pieces.append(digit.astype(jnp.bfloat16))
    levels = jnp.stack(pieces, axis=1)
    return levels.reshape((packed.shape[0] * 6, packed.shape[1]))


def prepare(stream, norm_gain, hadamard_table):
    mean_square = jnp.mean(stream * stream, axis=-1, keepdims=True)
    normed = stream * lax.rsqrt(mean_square + 1e-06) * norm_gain
    return rotate_blocks(normed, hadamard_table).astype(jnp.bfloat16)


def route_weights(router_logits):
    lifted = jax.nn.sigmoid(router_logits)
    return lifted / jnp.sum(lifted, axis=-1, keepdims=True)


def block_slots(expert_ids, block_rows, expert_count):
    expert_range = jnp.arange(expert_count, dtype=jnp.int32)
    member = jnp.sum(
        (expert_ids[:, :, None] == expert_range[None, None, :]).astype(jnp.int32), axis=1
    )
    blocks = member.reshape(-1, block_rows, expert_count)
    before = (jnp.cumsum(blocks, axis=1) - blocks).reshape(-1, expert_count)
    return jnp.take_along_axis(before, expert_ids, axis=1)


def place_rows(rotated, target, slot_count):
    slot_ids = jnp.arange(slot_count, dtype=jnp.int32)
    hits = (target[:, :, None] == slot_ids[None, None, :]).astype(jnp.bfloat16)
    placement = jnp.sum(hits, axis=1)
    return jnp.dot(placement.T, rotated, preferred_element_type=jnp.float32).astype(jnp.bfloat16)


def expert_rows(
    row_block, gate_levels, up_levels, down_levels, gate_row, up_row, down_row, hadamard_table
):
    feature_count = row_block.shape[1]
    gate_proj = jnp.dot(row_block, gate_levels, preferred_element_type=jnp.float32) * (
        gate_row * (1.0 / math.sqrt(level_variance * feature_count))
    )
    up_proj = jnp.dot(row_block, up_levels, preferred_element_type=jnp.float32) * (
        up_row * (1.0 / math.sqrt(level_variance * feature_count))
    )
    hidden = rotate_blocks(jax.nn.silu(gate_proj) * up_proj, hadamard_table).astype(jnp.bfloat16)
    whole_hidden = lax.all_gather(hidden, "tp", axis=1, tiled=True)
    hidden_count = whole_hidden.shape[1]
    expert_out = lax.dot_general(
        whole_hidden, down_levels, (((1,), (1,)), ((), ())), preferred_element_type=jnp.float32
    ) * (down_row * (1.0 / math.sqrt(level_variance * hidden_count)))
    return expert_out.astype(jnp.bfloat16)


def routed_shards(
    partials,
    residual,
    norm_gain,
    router_logits,
    expert_ids,
    gate_packed,
    up_packed,
    down_packed,
    gate_scale,
    up_scale,
    down_scale,
):
    tp_count = lax.axis_size("tp")
    ep_count = lax.axis_size("ep")
    tp_index = lax.axis_index("tp")
    block_tokens = residual.shape[0]
    half_rows = block_tokens // tp_count
    pick_count = expert_ids.shape[1]
    experts = ep_count * gate_packed.shape[0]
    capacity = max(2, half_rows * pick_count // experts)
    hadamard_table = hadamard(HB)
    gate_levels = unpack_levels(gate_packed[0])
    up_levels = unpack_levels(up_packed[0])
    down_levels = unpack_levels(down_packed[0])
    weights = route_weights(router_logits)
    slot_rank = block_slots(expert_ids, half_rows, experts)
    half_of_row = (jnp.arange(block_tokens, dtype=jnp.int32) // half_rows)[:, None]
    summed_rows = lax.psum_scatter(partials, "tp", scatter_dimension=1, tiled=True).astype(
        jnp.float32
    )
    own_resid = lax.dynamic_slice_in_dim(residual, tp_index * half_rows, half_rows, 0)
    stream = own_resid.astype(jnp.float32) + summed_rows[0]
    rotated = prepare(stream, norm_gain, hadamard_table)
    own_ids = lax.dynamic_slice_in_dim(expert_ids, tp_index * half_rows, half_rows, 0)
    own_slots = lax.dynamic_slice_in_dim(slot_rank, tp_index * half_rows, half_rows, 0)
    outgoing = place_rows(rotated, own_ids * capacity + own_slots, experts * capacity)
    outgoing = outgoing.reshape(experts, capacity, -1)
    arrived = lax.all_to_all(outgoing, "ep", split_axis=0, concat_axis=0, tiled=True)
    paired = lax.all_gather(arrived, "tp", axis=0, tiled=True)
    produced = expert_rows(
        paired.reshape(-1, paired.shape[2]),
        gate_levels,
        up_levels,
        down_levels,
        gate_scale[0],
        up_scale[0],
        down_scale[0],
        hadamard_table,
    )
    served = produced.reshape(tp_count, ep_count, arrived.shape[1], -1)
    returned = lax.all_to_all(served, "ep", split_axis=1, concat_axis=1, tiled=True)
    position = half_of_row * (experts * capacity) + expert_ids * capacity + slot_rank
    flat_back = returned.reshape(-1, returned.shape[-1])
    mixture = jnp.zeros((block_tokens, flat_back.shape[1]), jnp.float32)
    for pick in range(pick_count):
        fetched = jnp.take(flat_back, position[:, pick], axis=0)
        mixture = mixture + weights[:, pick : pick + 1] * fetched.astype(jnp.float32)
    arranged = mixture.reshape(tp_count, half_rows, -1)
    mixed = lax.all_to_all(
        arranged.astype(jnp.bfloat16), "tp", split_axis=0, concat_axis=2, tiled=True
    ).astype(arranged.dtype)
    return mixed[0].astype(jnp.bfloat16)


UNIT = 64
SPAN = 6 * UNIT
APART = ((0, None, 1), (0, None, 0), (1, None, 1), (1, None, 0))
ROUND = ((0, 0, 1), (0, 1, 0), (0, 0, 0), (0, 1, 1))
EXTRA = 128


def level_order():
    order = np.zeros((SPAN, SPAN), np.float32)
    for plane in range(6):
        for row in range(UNIT):
            order[6 * row + plane, plane * UNIT + row] = 1.0
    return order


def sign_blocks(count):
    indices = np.arange(HB)
    common = indices[:, None] & indices[None, :]
    parity = np.zeros((HB, HB), np.int64)
    for bit_pos in range(HB.bit_length() - 1):
        parity += (common >> bit_pos) & 1
    return np.kron(np.eye(count), 1.0 - 2.0 * (parity % 2)).astype(np.float32)


def fold(values, span):
    return jnp.concatenate(
        [values[:, i * span : (i + 1) * span] for i in range(values.shape[1] // span)], axis=0
    )


def unfold(values, rows):
    return jnp.concatenate(
        [values[i * rows : (i + 1) * rows] for i in range(values.shape[0] // rows)], axis=1
    )


def signed_product(values, signs):
    high = values.astype(jnp.bfloat16)
    low = (values - high.astype(jnp.float32)).astype(jnp.bfloat16)
    both = jnp.concatenate([high, low], axis=0)
    product = jnp.dot(both, signs, preferred_element_type=jnp.float32)
    rows = values.shape[0]
    return (product[:rows] + product[rows:]) * (1.0 / math.sqrt(HB))


def core_of(side):
    core = lax.axis_index("tp")
    return core if side == 0 else 1 - core


def own_rows(half, core):
    return pl.ds(pl.multiple_of(core * half, half), half)


def first_kernel(
    partial,
    resid,
    gain,
    signs,
    all_logits,
    all_ids,
    words,
    base,
    gain_out,
    signs_out,
    tail,
    words_out,
    rows_in,
    logits,
    ids,
    sems,
):
    copies = [
        pltpu.make_async_copy(partial, rows_in.at[0], sems.at[0]),
        pltpu.make_async_copy(resid, rows_in.at[1], sems.at[1]),
        pltpu.make_async_copy(gain, gain_out, sems.at[2]),
        pltpu.make_async_copy(signs, signs_out, sems.at[3]),
    ]
    small = [
        pltpu.make_async_copy(all_logits, logits, sems.at[4]),
        pltpu.make_async_copy(all_ids, ids, sems.at[5]),
    ]
    later = pltpu.make_async_copy(words, words_out, sems.at[6])
    for copy in small + copies + [later]:
        copy.start()
    for copy in small:
        copy.wait()
    lifted = jax.nn.sigmoid(logits[...])
    route = lifted / jnp.sum(lifted, axis=0, keepdims=True)
    picks, rows = route.shape
    expert = lax.broadcasted_iota(jnp.int32, (picks, rows), 0)
    spread = jnp.zeros((picks, rows), jnp.float32)
    for pick in range(picks):
        hit = expert == ids[pick : pick + 1, :]
        spread = spread + jnp.where(hit, route[pick : pick + 1, :], 0.0)
    high = spread.astype(jnp.bfloat16).astype(jnp.float32)
    blank = jnp.zeros((EXTRA - 2 * picks, rows), jnp.float32)
    columns = jnp.concatenate([high, spread - high, blank], axis=0)
    tail[...] = columns.T.astype(jnp.bfloat16)
    for copy in copies:
        copy.wait()
    base[...] = rows_in[1].astype(jnp.float32) + rows_in[0].astype(jnp.float32)
    later.wait()


def prep_kernel(side, base, other, gain, signs, tail, out):
    rows, features = out.shape[0], base.shape[1]
    at = own_rows(rows, core_of(side))
    stream = base[at, :] + other[at, :].astype(jnp.float32)
    mean_square = jnp.mean(stream * stream, axis=-1, keepdims=True)
    normed = stream * lax.rsqrt(mean_square + 1e-06) * gain[...].reshape(1, features)
    turned = signed_product(fold(normed, SPAN), signs[...])
    out[:, :features] = unfold(turned, rows).astype(jnp.bfloat16)
    out[:, features:] = tail[at, :]


def unpack_unit(words, out, at, columns):
    whole = words.astype(jnp.int32)
    for plane in range(6):
        digit = jnp.bitwise_and(jnp.right_shift(whole, 4 * plane), 15)
        level = digit.astype(jnp.float32) - 7.5
        out[pl.ds(at + plane * UNIT, UNIT), columns] = level.astype(jnp.bfloat16)


def unpack_all(packed, out, parts):
    def unit(index, carry):
        for source, columns in parts:
            words = packed[pl.ds(pl.multiple_of(index * UNIT, UNIT), UNIT), source]
            unpack_unit(words, out, pl.multiple_of(index * SPAN, SPAN), columns)
        return carry

    lax.fori_loop(0, packed.shape[0] // UNIT, unit, 0)


def unpack_gate_kernel(up, down, gate, out, up_out, down_out, sems):
    copies = [
        pltpu.make_async_copy(up, up_out, sems.at[0]),
        pltpu.make_async_copy(down, down_out, sems.at[1]),
    ]
    for copy in copies:
        copy.start()
    unpack_all(gate, out, ((slice(None), slice(None)),))
    for copy in copies:
        copy.wait()


def unpack_up_kernel(up, out):
    unpack_all(up, out, ((slice(None), slice(None)),))


def unpack_down_kernel(down, scale, order, out, row):
    half = down.shape[1] // 2
    core = lax.axis_index("tp")
    mine = pl.ds(pl.multiple_of(core * half, half), half)
    theirs = pl.ds(pl.multiple_of((1 - core) * half, half), half)
    unpack_all(down, out, ((mine, slice(0, half)), (theirs, slice(half, 2 * half))))
    rest = fold(jnp.broadcast_to(scale[...], (8, scale.shape[1])), SPAN)
    total = jnp.zeros(rest.shape, jnp.float32)
    for _ in range(3):
        term = rest.astype(jnp.bfloat16)
        rest = rest - term.astype(jnp.float32)
        total = total + jnp.dot(term, order[...], preferred_element_type=jnp.float32)
    row[...] = unfold(total, 8)


def slot_row(count, slot, side, part):
    at = slot if side is None else slot + core_of(side)
    return (2 * at + core_of(part)) * count


def hidden_kernel(slots, *refs):
    pieces, (gate, up, gate_row, up_row, signs, hidden, weight, rows_ref) = (
        refs[: len(slots)],
        refs[len(slots) :],
    )
    features = gate.shape[0]
    picks = lax.axis_size("ep")
    for piece, (slot, side, part) in zip(pieces, slots):
        count = piece.shape[0]
        lane = lax.broadcasted_iota(jnp.int32, (count, EXTRA), 1)
        picked = (lane < 2 * picks) & ((lane & (picks - 1)) == lax.axis_index("ep"))
        row = slot_row(count, slot, side, part)
        at = pl.ds(pl.multiple_of(row, count), count)
        rows_ref[at, :] = piece[:, :features]
        tail = jnp.where(picked, piece[:, features:].astype(jnp.float32), 0.0)
        total = jnp.sum(tail, axis=-1, keepdims=True)
        weight[at, :] = jnp.broadcast_to(total, (count, EXTRA))
    scale = 1.0 / math.sqrt(level_variance * features)
    rows = rows_ref[...]
    gate_proj = jnp.dot(rows, gate[...], preferred_element_type=jnp.float32)
    up_proj = jnp.dot(rows, up[...], preferred_element_type=jnp.float32)
    gate_proj, up_proj = gate_proj[: hidden.shape[0]], up_proj[: hidden.shape[0]]
    mixed = jax.nn.silu(gate_proj * (gate_row[...] * scale)) * (up_proj * (up_row[...] * scale))
    turned = signed_product(fold(mixed, 2 * HB), signs[...])
    hidden[...] = unfold(turned, mixed.shape[0])[: hidden.shape[0]].astype(jnp.bfloat16)


def down_kernel(mine, theirs, levels, down_row, weight, *outs):
    half = mine.shape[1]
    contract = (((1,), (1,)), ((), ()))
    produced = lax.dot_general(
        mine[...], levels[:, :half], contract, preferred_element_type=jnp.float32
    ) + lax.dot_general(
        theirs[...], levels[:, half:], contract, preferred_element_type=jnp.float32
    )
    scale = 1.0 / math.sqrt(level_variance * 2 * half)
    produced = produced * (down_row[:1, :] * scale) * weight[:, :1]
    rows = outs[0].shape[0]
    for index, out in enumerate(outs):
        out[...] = produced[index * rows : (index + 1) * rows]


def last_join_kernel(part, came, mine, other):
    for side, out in enumerate((mine, other)):
        at = own_rows(out.shape[0], core_of(side))
        out[...] = (part[at, :] + came[at, :].astype(jnp.float32)).astype(jnp.bfloat16)


def sum_rows(side, own, ahead, behind):
    at = own_rows(ahead.shape[0], core_of(side))
    came = ahead[...].astype(jnp.float32) + behind[...].astype(jnp.float32)
    return (own[at, :] + came).astype(jnp.bfloat16)


def give_kernel(own, ahead, behind, out):
    out[...] = sum_rows(1, own, ahead, behind)


def close_kernel(own, ahead, behind, given, order, out):
    rows, width = ahead.shape
    halves = (sum_rows(0, own, ahead, behind), given[...])
    folded = jnp.concatenate([fold(values, SPAN) for values in halves], axis=0)
    placed = jnp.dot(folded, order[...], preferred_element_type=jnp.float32).astype(jnp.bfloat16)
    height = placed.shape[0] // 2
    for side in range(2):
        column = pl.multiple_of(core_of(side) * width, width)
        part = unfold(placed[side * height : (side + 1) * height], rows)
        out[:, pl.ds(column, width)] = part


def on_chip(values):
    return pltpu.with_memory_space_constraint(values, pltpu.VMEM)


def whole_call(
    kernel, outs, name, *args, scratch=(), work=0, after=None, fetched=0, plain=False
):
    vmem = pl.BlockSpec(memory_space=pltpu.VMEM)
    specs = [pl.BlockSpec(memory_space=pltpu.HBM)] * fetched + [vmem] * (len(args) - fetched)
    stay = [pltpu.with_memory_space_constraint(a, pltpu.HBM) for a in args[:fetched]]
    args = (*stay, *args[fetched:])
    body = kernel
    if after is not None:
        specs, args = [pl.BlockSpec(memory_space=pl.ANY)] + specs, (after, *args)
        body = lambda first, *refs: kernel(*refs)
    return pl.pallas_call(
        body,
        in_specs=specs,
        out_specs=[vmem] * len(outs),
        out_shape=[(jax.ShapeDtypeStruct if plain else pltpu.VMEM)(*out) for out in outs],
        scratch_shapes=list(scratch),
        compiler_params=pltpu.CompilerParams(vmem_limit_bytes=12 << 20),
        cost_estimate=pl.CostEstimate(flops=work, bytes_accessed=0, transcendentals=0),
        name=name,
    )(*args)


def dense_shards(
    partials,
    residual,
    norm_gain,
    router_logits,
    expert_ids,
    gate_packed,
    up_packed,
    down_packed,
    gate_scale,
    up_scale,
    down_scale,
):
    ep_count = lax.axis_size("ep")
    tp_index = lax.axis_index("tp")
    block_rows, features = residual.shape
    half = block_rows // 2
    around = list(range(0, ep_count, 2)) + list(range(ep_count - 1, 0, -2))

    def device(spot, core):
        return around[spot % ep_count] * 2 + core

    def hop(values):
        spots = range(ep_count)
        pairs = [(device(s, 0), device(s + 1, 0)) for s in spots]
        pairs += [(device(s, 1), device(s - 1, 1)) for s in spots]
        return lax.ppermute(values, ("ep", "tp"), pairs)

    def turn_hop(values, step):
        pairs = [(device(s, c), device(s + step, c)) for s in range(ep_count) for c in range(2)]
        return lax.ppermute(values, ("ep", "tp"), pairs)

    def swap(values):
        return lax.ppermute(values, "tp", [(0, 1), (1, 0)])

    def own_half(values, other=False):
        at = (1 - tp_index if other else tp_index) * half
        return lax.dynamic_slice_in_dim(values, at, half, 0)

    turn = sign_blocks(SPAN // HB) @ level_order()
    turn = jnp.asarray(turn, jnp.bfloat16)
    turn_hidden = jnp.asarray(sign_blocks(2), jnp.bfloat16)
    order = jnp.asarray(level_order(), jnp.bfloat16)
    back = jnp.asarray(level_order().T, jnp.bfloat16)

    wide = features + EXTRA
    first = whole_call(
        first_kernel,
        [
            ((block_rows, features), jnp.float32),
            (norm_gain.shape, jnp.float32),
            (turn.shape, turn.dtype),
            ((block_rows, EXTRA), jnp.bfloat16),
            (gate_packed.shape[1:], jnp.float32),
        ],
        "first",
        partials[0],
        residual,
        norm_gain,
        turn,
        router_logits.T,
        expert_ids.T,
        gate_packed[0],
        fetched=7,
        scratch=[
            pltpu.VMEM((2, block_rows, features), jnp.bfloat16),
            pltpu.VMEM(router_logits.T.shape, jnp.float32),
            pltpu.VMEM(expert_ids.T.shape, jnp.int32),
            pltpu.SemaphoreType.DMA((7,)),
        ],
    )
    base, gain, turn, tail, gate_words = first
    other_partial = swap(partials[0])

    def prepared(side, after=None):
        (rows,) = whole_call(
            lambda *refs: prep_kernel(side, *refs),
            [((half, wide), jnp.bfloat16)],
            "prep",
            base,
            other_partial,
            gain,
            turn,
            tail,
            after=after,
        )
        return rows

    lead = [prepared(1)]
    follow = [prepared(0, after=lead[0])]

    packed_rows, columns = gate_packed.shape[1:]

    levels = ((6 * packed_rows, columns), jnp.bfloat16)
    gate, up_words, down_words = whole_call(
        unpack_gate_kernel,
        [levels, (up_packed.shape[1:], jnp.float32), (down_packed.shape[1:], jnp.float32)],
        "unpack_gate",
        up_packed[0],
        down_packed[0],
        on_chip(gate_words),
        fetched=2,
        scratch=[pltpu.SemaphoreType.DMA((2,))],
        after=follow[0],
        work=10**10,
    )
    down_rows, hidden_count = down_packed.shape[1:]
    down_features = 6 * down_rows

    def hold(values, *done):
        return lax.optimization_barrier((values, done))[0]

    def expert_hidden(pieces, slots, count, work=10**9):
        hidden, weight = whole_call(
            lambda *refs: hidden_kernel(slots, *refs),
            [
                ((block_rows * count, columns), jnp.bfloat16),
                ((block_rows * count, EXTRA), jnp.float32),
            ],
            "hidden_part",
            *pieces,
            on_chip(gate),
            on_chip(up),
            gate_scale,
            up_scale,
            turn_hidden,
            scratch=[pltpu.VMEM((max(2, count) * block_rows, features), jnp.bfloat16)],
            work=work,
        )
        return hidden, weight, swap(hidden)

    def expert_out(stage, after=None):
        hidden, weight, theirs = stage
        count = hidden.shape[0] // block_rows
        return whole_call(
            down_kernel,
            [((block_rows, down_features), jnp.float32)] * count,
            "down_part",
            hidden,
            theirs,
            on_chip(down),
            down_row,
            weight,
            work=2 * block_rows * count * hidden_count * down_features,
            after=after,
        )

    lead.append(hop(lead[0]))
    follow.append(hop(follow[0]))
    (up,) = whole_call(
        unpack_up_kernel, [levels], "unpack_up", on_chip(up_words), after=gate, work=10**10
    )
    lead[1] = hold(lead[1], gate)
    lead.append(hop(lead[1]))
    follow.append(hop(follow[1]))
    lead[2] = hold(lead[2], up)
    down, down_row = whole_call(
        unpack_down_kernel,
        [((down_features, hidden_count), jnp.bfloat16), ((8, down_features), jnp.float32)],
        "unpack_down",
        on_chip(down_words),
        down_scale,
        order,
        after=up,
        work=10**10,
    )
    lead.append(hop(lead[2]))
    follow.append(hop(follow[2]))

    def pieces(distance):
        ours = lead[distance], follow[distance]
        return [piece for own in ours for piece in (own, swap(own))]

    near = expert_hidden(pieces(1), ROUND, 2, work=10**9)
    lead[3] = hold(lead[3], near[1], down_row)
    lead.append(hop(lead[3]))
    beside = pieces(3)
    second = expert_hidden(hold(pieces(2), beside[1]), ROUND, 2, work=10**10)
    third = expert_hidden(beside, ROUND, 2, work=10**9)
    lead[4] = hold(lead[4], second[1], third[1])
    rows = [lead[4], swap(lead[4]), lead[0], follow[0]]
    edge = expert_hidden(hold(rows, third[1]), APART, 2, work=10**9)

    far = ep_count // 2

    def join(part, came):
        return (part + came.astype(jnp.float32)).astype(jnp.bfloat16)

    ahead, behind = {}, {}
    behind[3], ahead[3] = expert_out(third)
    edge, own = expert_out(edge, after=ahead[3])
    went_ahead = turn_hop(edge[:half].astype(jnp.bfloat16), 1)
    went_behind = turn_hop(edge[half:].astype(jnp.bfloat16), -1)
    behind[2], ahead[2] = expert_out(second, after=went_behind)
    behind[1], ahead[1] = expert_out(near, after=went_behind)
    for distance in range(far - 1, 1, -1):
        if distance == far - 1:
            send_ahead = jnp.concatenate(
                [
                    join(ahead[distance][:half], went_ahead),
                    ahead[distance][half:].astype(jnp.bfloat16),
                ],
                axis=0,
            )
            send_behind = jnp.concatenate(
                [
                    behind[distance][:half].astype(jnp.bfloat16),
                    join(behind[distance][half:], went_behind),
                ],
                axis=0,
            )
        else:
            send_ahead = join(ahead[distance], went_ahead)
            send_behind = join(behind[distance], went_behind)
        went_ahead, went_behind = turn_hop(send_ahead, 1), turn_hop(send_behind, -1)
    piece = ((half, down_features), jnp.bfloat16)

    def last_join(part, came):
        return whole_call(last_join_kernel, [piece] * 2, "last_join", part, came)

    mine_ahead, other_ahead = last_join(ahead[1], went_ahead)
    mine_behind, other_behind = last_join(behind[1], went_behind)
    other_ahead, other_behind = turn_hop(other_ahead, 1), turn_hop(other_behind, -1)
    mine_ahead, mine_behind = turn_hop(mine_ahead, 1), turn_hop(mine_behind, -1)
    (given,) = whole_call(give_kernel, [piece], "give", own, other_ahead, other_behind)
    (mixed,) = whole_call(
        close_kernel,
        [((half, features), jnp.bfloat16)],
        "close",
        own,
        mine_ahead,
        mine_behind,
        swap(given),
        back,
        plain=True,
    )
    return mixed


def solution(mesh):
    def shards(*args):
        experts = lax.axis_size("ep") * args[5].shape[0]
        every_row_everywhere = args[4].shape[1] == experts
        one_each = args[5].shape[0] == 1 and lax.axis_size("tp") == 2
        if every_row_everywhere and one_each and lax.axis_size("ep") == 8:
            return dense_shards(*args)
        return routed_shards(*args)

    return jax.shard_map(
        shards,
        mesh=mesh,
        in_specs=(
            P("tp", ("groups", "ep"), None),
            P(("groups", "ep"), None),
            P(),
            P(("groups", "ep"), None),
            P(("groups", "ep"), None),
            P("ep", None, "tp"),
            P("ep", None, "tp"),
            P("ep", "tp", None),
            P("ep", "tp"),
            P("ep", "tp"),
            P("ep", "tp"),
        ),
        out_specs=P(("groups", "ep", "tp"), None),
        check_vma=False,
    )
```

```python
import math

import jax
import jax.numpy as jnp
import numpy as np
from jax import lax
from jax.experimental import pallas as pl
from jax.experimental.pallas import tpu as pltpu
from jax.sharding import PartitionSpec as P

HB = 128


level_variance = 21.25
digit_powers = [1.0, 16.0, 256.0, 4096.0, 65536.0, 1048576.0]


def hadamard(table_order):
    indices = jnp.arange(table_order, dtype=jnp.int32)
    common_bits = jnp.bitwise_and(indices[:, None], indices[None, :])
    parity = jnp.zeros((table_order, table_order), jnp.int32)
    for bit_pos in range(table_order.bit_length() - 1):
        parity = parity + jnp.bitwise_and(jnp.right_shift(common_bits, bit_pos), 1)
    sign_table = 1 - 2 * (parity % 2)
    return sign_table.astype(jnp.float32) * (1.0 / math.sqrt(table_order))


def rotate_blocks(values, hadamard_table):
    feature_count = values.shape[-1]
    block_size = hadamard_table.shape[0]
    shaped = values.reshape(values.shape[:-1] + (feature_count // block_size, block_size))
    turned = jnp.einsum("rij,jk->rik", shaped, hadamard_table, precision=lax.Precision.HIGHEST)
    return turned.reshape(values.shape)


def unpack_levels(packed):
    pieces = []
    for power in digit_powers:
        digit = jnp.mod(jnp.floor(packed / power), 16.0) - 7.5
        pieces.append(digit.astype(jnp.bfloat16))
    levels = jnp.stack(pieces, axis=1)
    return levels.reshape((packed.shape[0] * 6, packed.shape[1]))


def prepare(stream, norm_gain, hadamard_table):
    mean_square = jnp.mean(stream * stream, axis=-1, keepdims=True)
    normed = stream * lax.rsqrt(mean_square + 1e-06) * norm_gain
    return rotate_blocks(normed, hadamard_table).astype(jnp.bfloat16)


def route_weights(router_logits):
    lifted = jax.nn.sigmoid(router_logits)
    return lifted / jnp.sum(lifted, axis=-1, keepdims=True)


def block_slots(expert_ids, block_rows, expert_count):
    expert_range = jnp.arange(expert_count, dtype=jnp.int32)
    member = jnp.sum(
        (expert_ids[:, :, None] == expert_range[None, None, :]).astype(jnp.int32), axis=1
    )
    blocks = member.reshape(-1, block_rows, expert_count)
    before = (jnp.cumsum(blocks, axis=1) - blocks).reshape(-1, expert_count)
    return jnp.take_along_axis(before, expert_ids, axis=1)


def place_rows(rotated, target, slot_count):
    slot_ids = jnp.arange(slot_count, dtype=jnp.int32)
    hits = (target[:, :, None] == slot_ids[None, None, :]).astype(jnp.bfloat16)
    placement = jnp.sum(hits, axis=1)
    return jnp.dot(placement.T, rotated, preferred_element_type=jnp.float32).astype(jnp.bfloat16)


def expert_rows(
    row_block, gate_levels, up_levels, down_levels, gate_row, up_row, down_row, hadamard_table
):
    feature_count = row_block.shape[1]
    gate_proj = jnp.dot(row_block, gate_levels, preferred_element_type=jnp.float32) * (
        gate_row * (1.0 / math.sqrt(level_variance * feature_count))
    )
    up_proj = jnp.dot(row_block, up_levels, preferred_element_type=jnp.float32) * (
        up_row * (1.0 / math.sqrt(level_variance * feature_count))
    )
    hidden = rotate_blocks(jax.nn.silu(gate_proj) * up_proj, hadamard_table).astype(jnp.bfloat16)
    whole_hidden = lax.all_gather(hidden, "tp", axis=1, tiled=True)
    hidden_count = whole_hidden.shape[1]
    expert_out = lax.dot_general(
        whole_hidden, down_levels, (((1,), (1,)), ((), ())), preferred_element_type=jnp.float32
    ) * (down_row * (1.0 / math.sqrt(level_variance * hidden_count)))
    return expert_out.astype(jnp.bfloat16)


def routed_shards(
    partials,
    residual,
    norm_gain,
    router_logits,
    expert_ids,
    gate_packed,
    up_packed,
    down_packed,
    gate_scale,
    up_scale,
    down_scale,
):
    tp_count = lax.axis_size("tp")
    ep_count = lax.axis_size("ep")
    tp_index = lax.axis_index("tp")
    block_tokens = residual.shape[0]
    half_rows = block_tokens // tp_count
    pick_count = expert_ids.shape[1]
    experts = ep_count * gate_packed.shape[0]
    capacity = max(2, half_rows * pick_count // experts)
    hadamard_table = hadamard(HB)
    gate_levels = unpack_levels(gate_packed[0])
    up_levels = unpack_levels(up_packed[0])
    down_levels = unpack_levels(down_packed[0])
    weights = route_weights(router_logits)
    slot_rank = block_slots(expert_ids, half_rows, experts)
    half_of_row = (jnp.arange(block_tokens, dtype=jnp.int32) // half_rows)[:, None]
    summed_rows = lax.psum_scatter(partials, "tp", scatter_dimension=1, tiled=True).astype(
        jnp.float32
    )
    own_resid = lax.dynamic_slice_in_dim(residual, tp_index * half_rows, half_rows, 0)
    stream = own_resid.astype(jnp.float32) + summed_rows[0]
    rotated = prepare(stream, norm_gain, hadamard_table)
    own_ids = lax.dynamic_slice_in_dim(expert_ids, tp_index * half_rows, half_rows, 0)
    own_slots = lax.dynamic_slice_in_dim(slot_rank, tp_index * half_rows, half_rows, 0)
    outgoing = place_rows(rotated, own_ids * capacity + own_slots, experts * capacity)
    outgoing = outgoing.reshape(experts, capacity, -1)
    arrived = lax.all_to_all(outgoing, "ep", split_axis=0, concat_axis=0, tiled=True)
    paired = lax.all_gather(arrived, "tp", axis=0, tiled=True)
    produced = expert_rows(
        paired.reshape(-1, paired.shape[2]),
        gate_levels,
        up_levels,
        down_levels,
        gate_scale[0],
        up_scale[0],
        down_scale[0],
        hadamard_table,
    )
    served = produced.reshape(tp_count, ep_count, arrived.shape[1], -1)
    returned = lax.all_to_all(served, "ep", split_axis=1, concat_axis=1, tiled=True)
    position = half_of_row * (experts * capacity) + expert_ids * capacity + slot_rank
    flat_back = returned.reshape(-1, returned.shape[-1])
    mixture = jnp.zeros((block_tokens, flat_back.shape[1]), jnp.float32)
    for pick in range(pick_count):
        fetched = jnp.take(flat_back, position[:, pick], axis=0)
        mixture = mixture + weights[:, pick : pick + 1] * fetched.astype(jnp.float32)
    arranged = mixture.reshape(tp_count, half_rows, -1)
    mixed = lax.all_to_all(
        arranged.astype(jnp.bfloat16), "tp", split_axis=0, concat_axis=2, tiled=True
    ).astype(arranged.dtype)
    return mixed[0].astype(jnp.bfloat16)


UNIT = 64
SPAN = 6 * UNIT
APART = ((0, None, 1), (0, None, 0), (1, None, 1), (1, None, 0))
ROUND = ((0, 0, 1), (0, 1, 0), (0, 0, 0), (0, 1, 1))
EXTRA = 128


def level_order():
    order = np.zeros((SPAN, SPAN), np.float32)
    for plane in range(6):
        for row in range(UNIT):
            order[6 * row + plane, plane * UNIT + row] = 1.0
    return order


def sign_blocks(count):
    indices = np.arange(HB)
    common = indices[:, None] & indices[None, :]
    parity = np.zeros((HB, HB), np.int64)
    for bit_pos in range(HB.bit_length() - 1):
        parity += (common >> bit_pos) & 1
    return np.kron(np.eye(count), 1.0 - 2.0 * (parity % 2)).astype(np.float32)


def fold(values, span):
    return jnp.concatenate(
        [values[:, i * span : (i + 1) * span] for i in range(values.shape[1] // span)], axis=0
    )


def unfold(values, rows):
    return jnp.concatenate(
        [values[i * rows : (i + 1) * rows] for i in range(values.shape[0] // rows)], axis=1
    )


def signed_product(values, signs):
    high = values.astype(jnp.bfloat16)
    low = (values - high.astype(jnp.float32)).astype(jnp.bfloat16)
    both = jnp.concatenate([high, low], axis=0)
    product = jnp.dot(both, signs, preferred_element_type=jnp.float32)
    rows = values.shape[0]
    return (product[:rows] + product[rows:]) * (1.0 / math.sqrt(HB))


def core_of(side):
    core = lax.axis_index("tp")
    return core if side == 0 else 1 - core


def own_rows(half, core):
    return pl.ds(pl.multiple_of(core * half, half), half)


def first_kernel(
    partial,
    resid,
    gain,
    signs,
    all_logits,
    all_ids,
    words,
    base,
    gain_out,
    signs_out,
    tail,
    words_out,
    rows_in,
    logits,
    ids,
    sems,
):
    copies = [
        pltpu.make_async_copy(partial, rows_in.at[0], sems.at[0]),
        pltpu.make_async_copy(resid, rows_in.at[1], sems.at[1]),
        pltpu.make_async_copy(gain, gain_out, sems.at[2]),
        pltpu.make_async_copy(signs, signs_out, sems.at[3]),
    ]
    small = [
        pltpu.make_async_copy(all_logits, logits, sems.at[4]),
        pltpu.make_async_copy(all_ids, ids, sems.at[5]),
    ]
    later = pltpu.make_async_copy(words, words_out, sems.at[6])
    for copy in small + copies + [later]:
        copy.start()
    for copy in small:
        copy.wait()
    lifted = jax.nn.sigmoid(logits[...])
    route = lifted / jnp.sum(lifted, axis=0, keepdims=True)
    picks, rows = route.shape
    expert = lax.broadcasted_iota(jnp.int32, (picks, rows), 0)
    spread = jnp.zeros((picks, rows), jnp.float32)
    for pick in range(picks):
        hit = expert == ids[pick : pick + 1, :]
        spread = spread + jnp.where(hit, route[pick : pick + 1, :], 0.0)
    high = spread.astype(jnp.bfloat16).astype(jnp.float32)
    blank = jnp.zeros((EXTRA - 2 * picks, rows), jnp.float32)
    columns = jnp.concatenate([high, spread - high, blank], axis=0)
    tail[...] = columns.T.astype(jnp.bfloat16)
    for copy in copies:
        copy.wait()
    base[...] = rows_in[1].astype(jnp.float32) + rows_in[0].astype(jnp.float32)
    later.wait()


def prep_kernel(side, base, other, gain, signs, tail, out):
    rows, features = out.shape[0], base.shape[1]
    at = own_rows(rows, core_of(side))
    stream = base[at, :] + other[at, :].astype(jnp.float32)
    mean_square = jnp.mean(stream * stream, axis=-1, keepdims=True)
    normed = stream * lax.rsqrt(mean_square + 1e-06) * gain[...].reshape(1, features)
    turned = signed_product(fold(normed, SPAN), signs[...])
    out[:, :features] = unfold(turned, rows).astype(jnp.bfloat16)
    out[:, features:] = tail[at, :]


def unpack_unit(words, out, at, columns):
    whole = words.astype(jnp.int32)
    for plane in range(6):
        digit = jnp.bitwise_and(jnp.right_shift(whole, 4 * plane), 15)
        level = digit.astype(jnp.float32) - 7.5
        out[pl.ds(at + plane * UNIT, UNIT), columns] = level.astype(jnp.bfloat16)


def unpack_all(packed, out, parts):
    def unit(index, carry):
        for source, columns in parts:
            words = packed[pl.ds(pl.multiple_of(index * UNIT, UNIT), UNIT), source]
            unpack_unit(words, out, pl.multiple_of(index * SPAN, SPAN), columns)
        return carry

    lax.fori_loop(0, packed.shape[0] // UNIT, unit, 0)


def unpack_gate_kernel(up, down, gate, out, up_out, down_out, sems):
    copies = [
        pltpu.make_async_copy(up, up_out, sems.at[0]),
        pltpu.make_async_copy(down, down_out, sems.at[1]),
    ]
    for copy in copies:
        copy.start()
    unpack_all(gate, out, ((slice(None), slice(None)),))
    for copy in copies:
        copy.wait()


def unpack_up_kernel(up, out):
    unpack_all(up, out, ((slice(None), slice(None)),))


def unpack_down_kernel(down, scale, order, out, row):
    half = down.shape[1] // 2
    core = lax.axis_index("tp")
    mine = pl.ds(pl.multiple_of(core * half, half), half)
    theirs = pl.ds(pl.multiple_of((1 - core) * half, half), half)
    unpack_all(down, out, ((mine, slice(0, half)), (theirs, slice(half, 2 * half))))
    rest = fold(jnp.broadcast_to(scale[...], (8, scale.shape[1])), SPAN)
    total = jnp.zeros(rest.shape, jnp.float32)
    for _ in range(3):
        term = rest.astype(jnp.bfloat16)
        rest = rest - term.astype(jnp.float32)
        total = total + jnp.dot(term, order[...], preferred_element_type=jnp.float32)
    row[...] = unfold(total, 8)


def slot_row(count, slot, side, part):
    at = slot if side is None else slot + core_of(side)
    return (2 * at + core_of(part)) * count


def hidden_kernel(slots, *refs):
    pieces, (gate, up, gate_row, up_row, signs, hidden, weight, rows_ref) = (
        refs[: len(slots)],
        refs[len(slots) :],
    )
    features = gate.shape[0]
    picks = lax.axis_size("ep")
    for piece, (slot, side, part) in zip(pieces, slots):
        count = piece.shape[0]
        lane = lax.broadcasted_iota(jnp.int32, (count, EXTRA), 1)
        picked = (lane < 2 * picks) & ((lane & (picks - 1)) == lax.axis_index("ep"))
        row = slot_row(count, slot, side, part)
        at = pl.ds(pl.multiple_of(row, count), count)
        rows_ref[at, :] = piece[:, :features]
        tail = jnp.where(picked, piece[:, features:].astype(jnp.float32), 0.0)
        total = jnp.sum(tail, axis=-1, keepdims=True)
        weight[at, :] = jnp.broadcast_to(total, (count, EXTRA))
    scale = 1.0 / math.sqrt(level_variance * features)
    rows = rows_ref[...]
    gate_proj = jnp.dot(rows, gate[...], preferred_element_type=jnp.float32)
    up_proj = jnp.dot(rows, up[...], preferred_element_type=jnp.float32)
    gate_proj, up_proj = gate_proj[: hidden.shape[0]], up_proj[: hidden.shape[0]]
    mixed = jax.nn.silu(gate_proj * (gate_row[...] * scale)) * (up_proj * (up_row[...] * scale))
    turned = signed_product(fold(mixed, 2 * HB), signs[...])
    hidden[...] = unfold(turned, mixed.shape[0])[: hidden.shape[0]].astype(jnp.bfloat16)


def down_kernel(mine, theirs, levels, down_row, weight, *outs):
    half = mine.shape[1]
    contract = (((1,), (1,)), ((), ()))
    produced = lax.dot_general(
        mine[...], levels[:, :half], contract, preferred_element_type=jnp.float32
    ) + lax.dot_general(
        theirs[...], levels[:, half:], contract, preferred_element_type=jnp.float32
    )
    scale = 1.0 / math.sqrt(level_variance * 2 * half)
    produced = produced * (down_row[:1, :] * scale) * weight[:, :1]
    start = 0
    for out in outs:
        out[...] = produced[start : start + out.shape[0]].astype(out.dtype)
        start += out.shape[0]


def last_join_kernel(part, came, mine, other):
    for side, out in enumerate((mine, other)):
        at = own_rows(out.shape[0], core_of(side))
        out[...] = (part[at, :] + came[at, :].astype(jnp.float32)).astype(jnp.bfloat16)


def sum_rows(side, own, ahead, behind):
    at = own_rows(ahead.shape[0], core_of(side))
    came = ahead[...].astype(jnp.float32) + behind[...].astype(jnp.float32)
    return (own[at, :] + came).astype(jnp.bfloat16)


def give_kernel(own, ahead, behind, out):
    out[...] = sum_rows(1, own, ahead, behind)


def close_kernel(own, ahead, behind, given, order, out):
    rows, width = ahead.shape
    halves = (sum_rows(0, own, ahead, behind), given[...])
    folded = jnp.concatenate([fold(values, SPAN) for values in halves], axis=0)
    placed = jnp.dot(folded, order[...], preferred_element_type=jnp.float32).astype(jnp.bfloat16)
    height = placed.shape[0] // 2
    for side in range(2):
        column = pl.multiple_of(core_of(side) * width, width)
        part = unfold(placed[side * height : (side + 1) * height], rows)
        out[:, pl.ds(column, width)] = part


def on_chip(values):
    return pltpu.with_memory_space_constraint(values, pltpu.VMEM)


def whole_call(
    kernel, outs, name, *args, scratch=(), work=0, after=None, fetched=0, plain=False
):
    vmem = pl.BlockSpec(memory_space=pltpu.VMEM)
    specs = [pl.BlockSpec(memory_space=pltpu.HBM)] * fetched + [vmem] * (len(args) - fetched)
    stay = [pltpu.with_memory_space_constraint(a, pltpu.HBM) for a in args[:fetched]]
    args = (*stay, *args[fetched:])
    body = kernel
    if after is not None:
        specs, args = [pl.BlockSpec(memory_space=pl.ANY)] + specs, (after, *args)
        body = lambda first, *refs: kernel(*refs)
    return pl.pallas_call(
        body,
        in_specs=specs,
        out_specs=[vmem] * len(outs),
        out_shape=[(jax.ShapeDtypeStruct if plain else pltpu.VMEM)(*out) for out in outs],
        scratch_shapes=list(scratch),
        compiler_params=pltpu.CompilerParams(vmem_limit_bytes=12 << 20),
        cost_estimate=pl.CostEstimate(flops=work, bytes_accessed=0, transcendentals=0),
        name=name,
    )(*args)


def dense_shards(
    partials,
    residual,
    norm_gain,
    router_logits,
    expert_ids,
    gate_packed,
    up_packed,
    down_packed,
    gate_scale,
    up_scale,
    down_scale,
):
    ep_count = lax.axis_size("ep")
    tp_index = lax.axis_index("tp")
    block_rows, features = residual.shape
    half = block_rows // 2
    around = list(range(0, ep_count, 2)) + list(range(ep_count - 1, 0, -2))

    def device(spot, core):
        return around[spot % ep_count] * 2 + core

    def hop(values):
        spots = range(ep_count)
        pairs = [(device(s, 0), device(s + 1, 0)) for s in spots]
        pairs += [(device(s, 1), device(s - 1, 1)) for s in spots]
        return lax.ppermute(values, ("ep", "tp"), pairs)

    def turn_hop(values, step):
        pairs = [(device(s, c), device(s + step, c)) for s in range(ep_count) for c in range(2)]
        return lax.ppermute(values, ("ep", "tp"), pairs)

    def swap(values):
        return lax.ppermute(values, "tp", [(0, 1), (1, 0)])

    def own_half(values, other=False):
        at = (1 - tp_index if other else tp_index) * half
        return lax.dynamic_slice_in_dim(values, at, half, 0)

    turn = sign_blocks(SPAN // HB) @ level_order()
    turn = jnp.asarray(turn, jnp.bfloat16)
    turn_hidden = jnp.asarray(sign_blocks(2), jnp.bfloat16)
    order = jnp.asarray(level_order(), jnp.bfloat16)
    back = jnp.asarray(level_order().T, jnp.bfloat16)

    wide = features + EXTRA
    first = whole_call(
        first_kernel,
        [
            ((block_rows, features), jnp.float32),
            (norm_gain.shape, jnp.float32),
            (turn.shape, turn.dtype),
            ((block_rows, EXTRA), jnp.bfloat16),
            (gate_packed.shape[1:], jnp.float32),
        ],
        "first",
        partials[0],
        residual,
        norm_gain,
        turn,
        router_logits.T,
        expert_ids.T,
        gate_packed[0],
        fetched=7,
        scratch=[
            pltpu.VMEM((2, block_rows, features), jnp.bfloat16),
            pltpu.VMEM(router_logits.T.shape, jnp.float32),
            pltpu.VMEM(expert_ids.T.shape, jnp.int32),
            pltpu.SemaphoreType.DMA((7,)),
        ],
    )
    base, gain, turn, tail, gate_words = first
    other_partial = swap(partials[0])

    def prepared(side, after=None):
        (rows,) = whole_call(
            lambda *refs: prep_kernel(side, *refs),
            [((half, wide), jnp.bfloat16)],
            "prep",
            base,
            other_partial,
            gain,
            turn,
            tail,
            after=after,
        )
        return rows

    lead = [prepared(1)]
    follow = [prepared(0, after=lead[0])]

    packed_rows, columns = gate_packed.shape[1:]

    levels = ((6 * packed_rows, columns), jnp.bfloat16)
    gate, up_words, down_words = whole_call(
        unpack_gate_kernel,
        [levels, (up_packed.shape[1:], jnp.float32), (down_packed.shape[1:], jnp.float32)],
        "unpack_gate",
        up_packed[0],
        down_packed[0],
        on_chip(gate_words),
        fetched=2,
        scratch=[pltpu.SemaphoreType.DMA((2,))],
        after=follow[0],
        work=10**10,
    )
    down_rows, hidden_count = down_packed.shape[1:]
    down_features = 6 * down_rows

    def hold(values, *done):
        return lax.optimization_barrier((values, done))[0]

    def expert_hidden(pieces, slots, count, work=10**9):
        hidden, weight = whole_call(
            lambda *refs: hidden_kernel(slots, *refs),
            [
                ((block_rows * count, columns), jnp.bfloat16),
                ((block_rows * count, EXTRA), jnp.float32),
            ],
            "hidden_part",
            *pieces,
            on_chip(gate),
            on_chip(up),
            gate_scale,
            up_scale,
            turn_hidden,
            scratch=[pltpu.VMEM((max(2, count) * block_rows, features), jnp.bfloat16)],
            work=work,
        )
        return hidden, weight, swap(hidden)

    def expert_out(stage, after=None, outs=None):
        hidden, weight, theirs = stage
        count = hidden.shape[0] // block_rows
        return whole_call(
            down_kernel,
            outs or [((block_rows, down_features), jnp.float32)] * count,
            "down_part",
            hidden,
            theirs,
            on_chip(down),
            down_row,
            weight,
            work=2 * block_rows * count * hidden_count * down_features,
            after=after,
        )

    lead.append(hop(lead[0]))
    follow.append(hop(follow[0]))
    (up,) = whole_call(
        unpack_up_kernel, [levels], "unpack_up", on_chip(up_words), after=gate, work=10**10
    )
    lead[1] = hold(lead[1], gate)
    lead.append(hop(lead[1]))
    follow.append(hop(follow[1]))
    lead[2] = hold(lead[2], up)
    down, down_row = whole_call(
        unpack_down_kernel,
        [((down_features, hidden_count), jnp.bfloat16), ((8, down_features), jnp.float32)],
        "unpack_down",
        on_chip(down_words),
        down_scale,
        order,
        after=up,
        work=10**10,
    )
    lead.append(hop(lead[2]))
    follow.append(hop(follow[2]))

    def pieces(distance):
        ours = lead[distance], follow[distance]
        return [piece for own in ours for piece in (own, swap(own))]

    near = expert_hidden(pieces(1), ROUND, 2, work=10**9)
    lead[3] = hold(lead[3], near[1], down_row)
    lead.append(hop(lead[3]))
    beside = pieces(3)
    second = expert_hidden(hold(pieces(2), beside[1]), ROUND, 2, work=10**10)
    third = expert_hidden(beside, ROUND, 2, work=10**9)
    lead[4] = hold(lead[4], second[1], third[1])
    rows = [lead[4], swap(lead[4]), lead[0], follow[0]]
    edge = expert_hidden(hold(rows, third[1]), APART, 2, work=10**9)

    far = ep_count // 2

    def join(part, came):
        return (part + came.astype(jnp.float32)).astype(jnp.bfloat16)

    ahead, behind = {}, {}
    behind[3], ahead[3] = expert_out(third)
    piece = ((half, down_features), jnp.bfloat16)
    edge_ahead, edge_behind, own = expert_out(
        edge, after=ahead[3], outs=[piece, piece, ((block_rows, down_features), jnp.float32)]
    )
    went_ahead = turn_hop(edge_ahead, 1)
    went_behind = turn_hop(edge_behind, -1)
    behind[2], ahead[2] = expert_out(second, after=went_behind)
    behind[1], ahead[1] = expert_out(near, after=went_behind)
    for distance in range(far - 1, 1, -1):
        if distance == far - 1:
            send_ahead = jnp.concatenate(
                [
                    join(ahead[distance][:half], went_ahead),
                    ahead[distance][half:].astype(jnp.bfloat16),
                ],
                axis=0,
            )
            send_behind = jnp.concatenate(
                [
                    behind[distance][:half].astype(jnp.bfloat16),
                    join(behind[distance][half:], went_behind),
                ],
                axis=0,
            )
        else:
            send_ahead = join(ahead[distance], went_ahead)
            send_behind = join(behind[distance], went_behind)
        went_ahead, went_behind = turn_hop(send_ahead, 1), turn_hop(send_behind, -1)
    piece = ((half, down_features), jnp.bfloat16)

    def last_join(part, came):
        return whole_call(last_join_kernel, [piece] * 2, "last_join", part, came)

    mine_ahead, other_ahead = last_join(ahead[1], went_ahead)
    mine_behind, other_behind = last_join(behind[1], went_behind)
    other_ahead, other_behind = turn_hop(other_ahead, 1), turn_hop(other_behind, -1)
    mine_ahead, mine_behind = turn_hop(mine_ahead, 1), turn_hop(mine_behind, -1)
    (given,) = whole_call(give_kernel, [piece], "give", own, other_ahead, other_behind)
    (mixed,) = whole_call(
        close_kernel,
        [((half, features), jnp.bfloat16)],
        "close",
        own,
        mine_ahead,
        mine_behind,
        swap(given),
        back,
        plain=True,
    )
    return mixed


def solution(mesh):
    def shards(*args):
        experts = lax.axis_size("ep") * args[5].shape[0]
        every_row_everywhere = args[4].shape[1] == experts
        one_each = args[5].shape[0] == 1 and lax.axis_size("tp") == 2
        if every_row_everywhere and one_each and lax.axis_size("ep") == 8:
            return dense_shards(*args)
        return routed_shards(*args)

    return jax.shard_map(
        shards,
        mesh=mesh,
        in_specs=(
            P("tp", ("groups", "ep"), None),
            P(("groups", "ep"), None),
            P(),
            P(("groups", "ep"), None),
            P(("groups", "ep"), None),
            P("ep", None, "tp"),
            P("ep", None, "tp"),
            P("ep", "tp", None),
            P("ep", "tp"),
            P("ep", "tp"),
            P("ep", "tp"),
        ),
        out_specs=P(("groups", "ep", "tp"), None),
        check_vma=False,
    )
```
